32 devices in a mesh: gx: 8 (over y, x, core), gy: 4 (over z).
Axes of the slice: x: 2, y: 2, z: 4, core: 2. Of those that a mesh axis runs over, the one named last changes fastest.
Arguments:
- velocity: float32 [3, 128, 64, 256], P(None, 'gx', 'gy'), may hold values from -6 to 6
- weights: bfloat16 [8, 4, 8, 3, 64, 128], P('gx', 'gy'), may hold values from 0 to 0.015625
- targets: bfloat16 [8, 4, 8, 3, 192], P('gx', 'gy'), may hold values from -5 to 5
- owner_list: int32 [8, 4, 8, 3], P('gx', 'gy'), may hold values from -1 to 511, as said below
- slot_patch: int32 [8, 4, 8, 3], P('gx', 'gy'), may hold values from -1 to 511, as said below
Outputs:
- velocity_new: float32 [3, 128, 64, 256], P(None, 'gx', 'gy')
- marker_force: float32 [8, 4, 8, 3, 192], P('gx', 'gy')
The draws below stay inside these ranges and needn't reach their ends.
Inputs may be any that keep to these rules, and one draw needn't show every extreme that they name: owner_list[i, j, d, s] is the patch of tile (d, j) that slot s of owner (i, j) addresses, or -1 for an empty slot; every slot from every owner toward the footprint tiles d in [2, 2 + max(1, 1)), j in [1, 1 + max(1, 1)) is live; several slots may address one patch. slot_patch[d, j, i, s] = owner_list[i, j, d, s].
All inputs are finite; a program needn't handle non-finite values.
Results may differ from the reference program's by a relative error of at most 0.0003.
Values may be sent and summed in bfloat16 or wider, within the bound.
No kernel may reach another device: no remote copies, remote signals or barrier semaphores. Data moves between devices by JAX's collectives and lax.ppermute only.
A program may use at most 128 MiB of HBM per device.

```python
import jax
import jax.numpy as jnp
from jax import lax

CX = 16
CY = 16
NZ = 256
B = 64
SLOTS = 3
NBX = 8
NBY = 4
NX = 128
NY = 64
PATCHES = 512


def routing(key):
    inner = jax.random.fold_in(key, 7)
    first, second = jax.random.split(inner)
    shape = (NBX, NBY, NBX, SLOTS)
    patch_ids = jax.random.randint(first, shape, 0, PATCHES)
    chance = jax.random.randint(second, shape, 0, 4)
    dest_d = jnp.arange(NBX)[None, None, :, None]
    rows_j = jnp.arange(NBY)[None, :, None, None]
    start_d = NBX // 4
    start_j = NBY // 4
    footprint = (dest_d >= start_d) & (dest_d < start_d + max(1, NBX // 8)) & (rows_j >= start_j) & (rows_j < start_j + max(1, NBY // 4))
    live = footprint | (chance == 0)
    live = live.at[0, 0, 0, 1].set(False)
    patch_ids = patch_ids.at[0, start_j, start_d, 0].set(PATCHES - 1)
    return jnp.where(live, patch_ids, -1).astype(jnp.int32)


def draw_owner_list(key, part):
    return routing(key)


def draw_slot_patch(key, part):
    return jnp.transpose(routing(key), (2, 1, 0, 3))


def levels(key, shape, cuts, low, high):
    def one(position, shards_of):
        draws = jax.random.uniform(jax.random.fold_in(jax.random.fold_in(key, 6), position), (shards_of,), jnp.float32, low / len(cuts), high / len(cuts))
        return jnp.repeat(jnp.exp(draws), shape[position] // shards_of).reshape((-1,) + (1,) * (len(shape) - position - 1))

    level = one(*cuts[0])
    for cut in cuts[1:]:
        level = level * one(*cut)
    return level


def normal_values(rng, extent, scale, bound, cuts=(), kind=jnp.bfloat16):
    result = jax.random.normal(rng, extent, jnp.float32) * scale
    if len(cuts) > 0:
        result = levels(rng, extent, cuts, -0.22, 0.18) * result
    return jnp.clip(result, min=-bound, max=bound).astype(kind)


def setup_inputs(seed: int = 0) -> dict:
    streams_of = jax.random.split(jax.random.key(seed), 6)
    velocity = normal_values(streams_of[0], (3, NX, NY, NZ), 1.0, 6.0, ((1, 8), (2, 4)), jnp.float32)
    weights = jnp.clip(0.015625 * jax.random.uniform(streams_of[1], (NBX, NBY, NBX, SLOTS, B, 128), jnp.float32) ** levels(streams_of[1], (NBX, NBY, NBX, SLOTS, B, 128), ((0, 8), (1, 4)), -0.2, 0.2), 0.0, 0.015625).astype(jnp.bfloat16)
    targets = normal_values(streams_of[2], (NBX, NBY, NBX, 3, SLOTS * B), 1.0, 5.0, ((0, 8), (1, 4)))
    owner_list = draw_owner_list(jax.random.fold_in(streams_of[5], 71), 0)
    slot_patch = draw_slot_patch(jax.random.fold_in(streams_of[5], 71), 0)
    return {"velocity": velocity, "weights": weights, "targets": targets, "owner_list": owner_list, "slot_patch": slot_patch}


time_step = 0.05
viscosity = 0.5
spread_gain = 0.5


def advance(padded):
    center = padded[:, 1:-1, 1:-1, 1:-1]
    fore_cell = padded[:, 2:, 1:-1, 1:-1]
    back_cell = padded[:, :-2, 1:-1, 1:-1]
    right_cell = padded[:, 1:-1, 2:, 1:-1]
    left_cell = padded[:, 1:-1, :-2, 1:-1]
    top_cell = padded[:, 1:-1, 1:-1, 2:]
    bottom_cell = padded[:, 1:-1, 1:-1, :-2]
    laplace = fore_cell + back_cell + right_cell + left_cell + top_cell + bottom_cell - 6.0 * center
    advect = center[0:1] * (fore_cell - back_cell) * 0.5 + center[1:2] * (right_cell - left_cell) * 0.5 + center[2:3] * (top_cell - bottom_cell) * 0.5
    return center + time_step * (viscosity * laplace - advect)


def reference(velocity, weights, targets, owner_list, slot_patch):
    padded = jnp.pad(velocity, ((0, 0), (1, 1), (1, 1), (0, 0)), mode="wrap")
    padded = jnp.pad(padded, ((0, 0), (0, 0), (0, 0), (1, 1)))
    predicted = advance(padded)
    lowered = predicted.astype(jnp.bfloat16)
    tiles = lowered.reshape(3, NBX, CX // 4, 4, NBY, CX // 4 * 0 + CY // 4, 4, NZ // 8, 8)
    tiles = jnp.transpose(tiles, (1, 4, 2, 5, 7, 0, 3, 6, 8)).reshape(NBX, NBY, PATCHES, 3, 128)
    rows_j = jnp.arange(NBY, dtype=jnp.int32)[:, None, None]
    dest_d = jnp.arange(NBX, dtype=jnp.int32)[None, :, None]
    incoming_all = jnp.transpose(slot_patch, (2, 1, 0, 3))

    def step(carry, inputs):
        w_owner, t_owner, id_owner, id_incoming = inputs
        own_live = id_owner >= 0
        in_live = id_incoming >= 0
        safe = jnp.maximum(id_incoming, 0).astype(jnp.int32)
        chosen = tiles[dest_d, rows_j, safe]
        interp = jnp.einsum("jdsbp,jdscp->jdscb", w_owner.astype(jnp.float32), chosen.astype(jnp.float32))
        target = jnp.transpose(t_owner.astype(jnp.float32).reshape(NBY, NBX, 3, SLOTS, B), (0, 1, 3, 2, 4))
        force = jnp.where(own_live[:, :, :, None, None], (target - interp) / time_step, 0.0)
        force_low = force.astype(jnp.bfloat16)
        spread = jnp.einsum("jdscb,jdsbp->jdscp", force_low.astype(jnp.float32), w_owner.astype(jnp.float32))
        spread = jnp.where(in_live[:, :, :, None, None], spread, 0.0)
        carry = carry.at[dest_d, rows_j, safe].add(spread)
        out_force = jnp.transpose(force, (0, 1, 3, 2, 4)).reshape(NBY, NBX, 3, SLOTS * B)
        return carry, out_force

    start = jnp.zeros((NBX, NBY, PATCHES, 3, 128), jnp.float32)
    field, marker_force = lax.scan(step, start, (weights, targets, owner_list, incoming_all))
    field = field.reshape(NBX, NBY, CX // 4, CY // 4, NZ // 8, 3, 4, 4, 8)
    field = jnp.transpose(field, (5, 0, 2, 6, 1, 3, 7, 4, 8)).reshape(3, NBX * CX, NBY * CY, NZ)
    velocity_new = predicted + time_step * spread_gain * field
    return velocity_new, marker_force
```

```python
import functools

import jax
import jax.numpy as jnp
from jax import lax
from jax.experimental import pallas as pl
from jax.experimental.pallas import tpu as pltpu
from jax.sharding import PartitionSpec as P

time_step = 0.05
viscosity = 0.5
spread_gain = 0.5

VMEM = pltpu.VMEM
F32 = jnp.float32
BF16 = jnp.bfloat16


def each(count, body):
    if count <= 8:
        for i in range(count):
            body(i)
    else:

        def step(i, carry):
            body(i)
            return carry

        lax.fori_loop(0, count, step, 0)


def pack_kernel(dims, vel, w, t, chunk, x_first, x_last, y_first, y_last, held, rows, packed, sems):
    size_x, size_y, count_d, width = dims
    move_w = pltpu.make_async_copy(w, chunk.at[:, pl.ds(0, width), :], sems.at[0])
    halves = held.shape[0]
    moves = [
        pltpu.make_async_copy(vel.at[:, pl.ds(part * 128, 128)], held.at[part], sems.at[2 + part])
        for part in range(halves)
    ]
    for move in moves:
        move.start()
    move_w.start()
    rows[...] = jnp.zeros_like(rows)

    def one(i):
        values = t[i].astype(F32)
        rows[i, 0:3, :] = values[:, 0:128]
        rows[i, 8:11, 0 : width - 128] = values[:, 128:width]

    each(count_d, one)
    packed[...] = rows[...].astype(BF16)
    move_t = pltpu.make_async_copy(packed, chunk.at[:, pl.ds(width, 16), :], sems.at[1])
    move_t.start()
    plane = size_x * size_y
    for part in range(halves):
        moves[part].wait()
        lanes = pl.ds(part * 128, 128)
        for c in range(3):
            x_first[c, :, lanes] = held[part, pl.ds(c * plane, size_y), :]
            x_last[c, :, lanes] = held[part, pl.ds(c * plane + plane - size_y, size_y), :]
            y_first[c, :, lanes] = held[part, pl.ds(c * plane, size_x, stride=size_y), :]
            y_last[c, :, lanes] = held[part, pl.ds(c * plane + size_y - 1, size_x, stride=size_y), :]
    move_t.wait()
    move_w.wait()


def main_kernel(
    dims, slots, vel, x_before, x_after, y_before, y_after, chunk, out, force_out,
    held, field, blocks, chosen, sems,
):
    size_x, size_y, size_z, count_d, count_s, width = dims
    move_v = pltpu.make_async_copy(vel, held, sems.at[0])
    move_w = pltpu.make_async_copy(chunk, blocks, sems.at[1])
    move_v.start()
    move_w.start()
    columns_y = size_y // 4
    layers_z = size_z // 8
    markers = width // count_s

    row = lax.broadcasted_iota(jnp.int32, (size_y, size_z), 0)
    col = lax.broadcasted_iota(jnp.int32, (size_y, size_z), 1)
    move_v.wait()
    for x in range(size_x):
        center, fore, back, right, left, top, bottom = [], [], [], [], [], [], []
        for c in range(3):
            base = (c * size_x + x) * size_y
            here = held[pl.ds(base, size_y), :]
            center.append(here)
            fore.append(x_after[c] if x == size_x - 1 else held[pl.ds(base + size_y, size_y), :])
            back.append(x_before[c] if x == 0 else held[pl.ds(base - size_y, size_y), :])
            right.append(
                jnp.where(row == size_y - 1, y_after[c, pl.ds(x, 1), :], pltpu.roll(here, size_y - 1, 0))
            )
            left.append(jnp.where(row == 0, y_before[c, pl.ds(x, 1), :], pltpu.roll(here, 1, 0)))
            top.append(jnp.where(col == size_z - 1, 0.0, pltpu.roll(here, size_z - 1, 1)))
            bottom.append(jnp.where(col == 0, 0.0, pltpu.roll(here, 1, 1)))
        for c in range(3):
            laplace = fore[c] + back[c] + right[c] + left[c] + top[c] + bottom[c] - 6.0 * center[c]
            advect = (
                center[0] * (fore[c] - back[c]) * 0.5
                + center[1] * (right[c] - left[c]) * 0.5
                + center[2] * (top[c] - bottom[c]) * 0.5
            )
            base = (c * size_x + x) * size_y
            field[pl.ds(base, size_y), :] = center[c] + time_step * (viscosity * laplace - advect)

    lane = lax.broadcasted_iota(jnp.int32, (8, 128), 1)
    sub = lax.broadcasted_iota(jnp.int32, (8, 128), 0)
    lane_x = lane // 32
    sub_half = jnp.where((lane // 8) % 4 == sub % 4, sub // 4, -1)
    odd = sub % 2 == 1
    upper = sub % 4 >= 2

    def place(i, s):
        safe = jnp.maximum(slots[0, 0, i, s], 0)
        qx = safe // (columns_y * layers_z)
        qy = safe // layers_z % columns_y
        qz = safe % layers_z
        first = qx * (4 * size_y) + (qy // 2) * 8
        half = qy % 2
        lanes = pl.ds(pl.multiple_of((qz // 16) * 128, 128), 128)
        shift = 8 * (qz % 16)
        return first, half, lanes, shift

    def spot(first, c, ax, lanes):
        return pl.ds(pl.multiple_of(first + (c * size_x + ax) * size_y, 8), 8), lanes

    def gather(i):
        for s in range(count_s):
            first, half, lanes, shift = place(i, s)
            wanted = sub_half == half
            picked = jnp.zeros((8, 128), F32)
            for c in range(3):
                merged = None
                for ax in range(4):
                    piece = field[spot(first, c, ax, lanes)]
                    piece = pltpu.roll(piece, (128 + 32 * ax - shift) % 128, 1)
                    merged = piece if ax == 0 else jnp.where(lane_x == ax, piece, merged)
                merged = jnp.where(odd, pltpu.roll(merged, 8, 1), merged)
                merged = jnp.where(upper, pltpu.roll(merged, 16, 1), merged)
                line = jnp.sum(jnp.where(wanted, merged, 0.0), axis=0, keepdims=True)
                picked = jnp.where(sub == c, line, picked)
            chosen[i, pl.ds(8 * s, 8), :] = picked

    each(count_d, gather)
    move_w.wait()
    slot_of = lax.broadcasted_iota(jnp.int32, (8, width), 1) // markers

    def force_and_spread(i):
        block_w = blocks[i, 0:width, :]
        tail = blocks[i, width : width + 16, :].astype(F32)
        target = jnp.concatenate([tail[0:8, :], tail[8:16, 0 : width - 128]], axis=1)
        product = lax.dot_general(
            chosen[i].astype(BF16), block_w, (((1,), (1,)), ((), ())), preferred_element_type=F32
        )
        interp = product[0:8]
        live = jnp.full((8, width), slots[0, 0, i, 0], jnp.int32)
        for s in range(1, count_s):
            interp = jnp.where(slot_of == s, product[8 * s : 8 * s + 8], interp)
            live = jnp.where(slot_of == s, slots[0, 0, i, s], live)
        force = jnp.where(live >= 0, (target - interp) / time_step, 0.0)
        force_out[i] = force[0:3, :]
        rows = jnp.concatenate([jnp.where(slot_of == s, force, 0.0) for s in range(count_s)], axis=0)
        chosen[i] = jnp.dot(rows.astype(BF16), block_w, preferred_element_type=F32)

    each(count_d, force_and_spread)

    def scatter(i):
        for s in range(count_s):
            first, half, lanes, shift = place(i, s)
            wanted = sub_half == half
            rows = chosen[i, pl.ds(8 * s, 8), :] * (time_step * spread_gain)
            for c in range(3):
                line = jnp.where(wanted, rows[c : c + 1, :], 0.0)
                line = jnp.where(odd, pltpu.roll(line, 120, 1), line)
                line = jnp.where(upper, pltpu.roll(line, 112, 1), line)
                for ax in range(4):
                    piece = jnp.where(lane_x == ax, line, 0.0)
                    piece = pltpu.roll(piece, (128 + shift - 32 * ax) % 128, 1)
                    at = spot(first, c, ax, lanes)
                    field[at] = field[at] + piece

    each(count_d, scatter)
    pltpu.sync_copy(field, out)


def shards(velocity, weights, targets, owner_list, slot_patch):
    size_x, size_y, size_z = velocity.shape[1:]
    count_d, count_s, markers = weights.shape[2:5]
    width = count_s * markers
    cells = 3 * size_x * size_y
    vel = velocity.reshape(cells, size_z)
    block_w = weights.reshape(count_d, width, 128)
    anywhere = pl.BlockSpec(memory_space=pl.ANY)
    inside = pl.BlockSpec(memory_space=VMEM)
    face_x = jax.ShapeDtypeStruct((3, size_y, size_z), F32)
    face_y = jax.ShapeDtypeStruct((3, size_x, size_z), F32)
    chunk, x_first, x_last, y_first, y_last = pl.pallas_call(
        functools.partial(pack_kernel, (size_x, size_y, count_d, width)),
        out_shape=(
            jax.ShapeDtypeStruct((count_d, width + 16, 128), BF16),
            face_x, face_x, face_y, face_y,
        ),
        in_specs=[anywhere, anywhere, inside],
        out_specs=(anywhere, inside, inside, inside, inside),
        scratch_shapes=[
            VMEM((size_z // 128, cells, 128), F32),
            VMEM((count_d, 16, 128), F32),
            VMEM((count_d, 16, 128), BF16),
            pltpu.SemaphoreType.DMA((2 + size_z // 128,)),
        ],
        compiler_params=pltpu.CompilerParams(vmem_limit_bytes=16 * 2**20),
        name="pack",
    )(vel, block_w, targets.reshape(count_d, 3, width))

    def ring(x, axis, step):
        size = lax.axis_size(axis)
        return lax.ppermute(x, axis, [(i, (i + step) % size) for i in range(size)])

    y_before = ring(y_last, "gy", 1)
    y_after = ring(y_first, "gy", -1)
    x_before = ring(x_last, "gx", 1)
    x_after = ring(x_first, "gx", -1)
    arrived = lax.all_to_all(chunk, "gx", split_axis=0, concat_axis=0, tiled=True)
    out, force = pl.pallas_call(
        functools.partial(main_kernel, (size_x, size_y, size_z, count_d, count_s, width)),
        out_shape=(
            jax.ShapeDtypeStruct((cells, size_z), F32),
            jax.ShapeDtypeStruct((count_d, 3, width), F32),
        ),
        in_specs=[
            pl.BlockSpec(memory_space=pltpu.SMEM),
            anywhere, inside, inside, inside, inside, anywhere,
        ],
        out_specs=(anywhere, inside),
        scratch_shapes=[
            VMEM((cells, size_z), F32),
            VMEM((cells, size_z), F32),
            VMEM((count_d, width + 16, 128), BF16),
            VMEM((count_d, 8 * count_s, 128), F32),
            pltpu.SemaphoreType.DMA((2,)),
        ],
        compiler_params=pltpu.CompilerParams(vmem_limit_bytes=16 * 2**20),
        name="main",
    )(slot_patch, vel, x_before, x_after, y_before, y_after, arrived)
    returned = lax.all_to_all(force, "gx", split_axis=0, concat_axis=0, tiled=True)
    return out.reshape(velocity.shape), returned[None, None]


def solution(mesh):
    return jax.shard_map(
        shards,
        mesh=mesh,
        in_specs=(
            P(None, "gx", "gy", None),
            P("gx", "gy", None, None, None, None),
            P("gx", "gy", None, None, None),
            P("gx", "gy", None, None),
            P("gx", "gy", None, None),
        ),
        out_specs=(P(None, "gx", "gy", None), P("gx", "gy", None, None, None)),
        check_vma=False,
    )
```

```python
import functools

import jax
import jax.numpy as jnp
from jax import lax
from jax.experimental import pallas as pl
from jax.experimental.pallas import tpu as pltpu
from jax.sharding import PartitionSpec as P

time_step = 0.05
viscosity = 0.5
spread_gain = 0.5

VMEM = pltpu.VMEM
F32 = jnp.float32
BF16 = jnp.bfloat16


def each(count, body, flat=False):
    if flat or count == 1:
        for i in range(count):
            body(i)
    else:

        def step(i, carry):
            body(i)
            return carry

        lax.fori_loop(0, count, step, 0)


def pack_kernel(dims, vel, w, t, chunk, x_first, x_last, y_first, y_last, held, rows, sems):
    size_x, size_y, count_d, width = dims
    halves = held.shape[0]
    moves = [
        pltpu.make_async_copy(vel.at[:, pl.ds(part * 128, 128)], held.at[part], sems.at[1 + part])
        for part in range(halves)
    ]
    for move in moves:
        move.start()
    move_w = pltpu.make_async_copy(w, chunk.at[:, pl.ds(0, width), :], sems.at[0])
    move_w.start()
    rows[...] = jnp.zeros_like(rows)
    rest = jnp.zeros((count_d, 256 - width), F32)
    for c in range(3):
        values = t[c].astype(F32)
        rows[pl.ds(c, count_d, stride=16), :] = values[:, 0:128]
        rows[pl.ds(8 + c, count_d, stride=16), :] = jnp.concatenate([values[:, 128:width], rest], axis=1)
    chunk[:, width : width + 16, :] = rows[...].astype(BF16).reshape(count_d, 16, 128)
    plane = size_x * size_y
    for part in range(halves):
        moves[part].wait()
        lanes = pl.ds(part * 128, 128)
        for c in range(3):
            x_first[c, :, lanes] = held[part, pl.ds(c * plane, size_y), :]
            x_last[c, :, lanes] = held[part, pl.ds(c * plane + plane - size_y, size_y), :]
            y_first[c, :, lanes] = held[part, pl.ds(c * plane, size_x, stride=size_y), :]
            y_last[c, :, lanes] = held[part, pl.ds(c * plane + size_y - 1, size_x, stride=size_y), :]
    move_w.wait()


def split(x, size):
    if size & (size - 1) == 0:
        return lax.shift_right_logical(x, size.bit_length() - 1), x & (size - 1)
    return lax.div(x, size), lax.rem(x, size)


def main_kernel(
    dims, slots, vel, x_before, x_after, y_before, y_after, blocks, out, force_out,
    field, stage, chosen,
):
    size_x, size_y, size_z, count_d, count_s, width = dims
    columns_y = size_y // 4
    layers_z = size_z // 8
    markers = width // count_s
    cells = 3 * size_x * size_y
    halves = size_z // 128

    row = lax.broadcasted_iota(jnp.int32, (size_y, size_z), 0)
    col = lax.broadcasted_iota(jnp.int32, (size_y, size_z), 1)

    def stencil(x):
        center, fore, back, right, left, top, bottom = [], [], [], [], [], [], []
        for c in range(3):
            base = (c * size_x + x) * size_y
            here = vel[pl.ds(base, size_y), :]
            center.append(here)
            fore.append(x_after[c] if x == size_x - 1 else vel[pl.ds(base + size_y, size_y), :])
            back.append(x_before[c] if x == 0 else vel[pl.ds(base - size_y, size_y), :])
            right.append(
                jnp.where(row == size_y - 1, y_after[c, pl.ds(x, 1), :], pltpu.roll(here, size_y - 1, 0))
            )
            left.append(jnp.where(row == 0, y_before[c, pl.ds(x, 1), :], pltpu.roll(here, 1, 0)))
            top.append(jnp.where(col == size_z - 1, 0.0, pltpu.roll(here, size_z - 1, 1)))
            bottom.append(jnp.where(col == 0, 0.0, pltpu.roll(here, 1, 1)))
        for c in range(3):
            laplace = fore[c] + back[c] + right[c] + left[c] + top[c] + bottom[c] - 6.0 * center[c]
            advect = (
                center[0] * (fore[c] - back[c]) * 0.5
                + center[1] * (right[c] - left[c]) * 0.5
                + center[2] * (top[c] - bottom[c]) * 0.5
            )
            base = 8 + (c * size_x + x) * size_y
            result = center[c] + time_step * (viscosity * laplace - advect)
            for part in range(halves):
                field[part, pl.ds(base, size_y), :] = result[:, part * 128 : part * 128 + 128]

    each(size_x, stencil, True)

    lane = lax.broadcasted_iota(jnp.int32, (8, 128), 1)
    sub = lax.broadcasted_iota(jnp.int32, (8, 128), 0)
    low_lane = lane < 64
    low_sub = sub < 4
    group = 8 if count_d % 8 == 0 else 1
    lines = group * count_s * 8

    def shifts(rows, columns, piece_axis):
        shape = (rows, columns)
        piece = lax.broadcasted_iota(jnp.int32, shape, piece_axis)
        place = lax.broadcasted_iota(jnp.int32, shape, 1 - piece_axis) & 127
        m = piece & 127
        hit = ((m & 63) < 8) & (place == m + 8 * lax.shift_right_logical(piece, 7))
        return jnp.where(hit, 1.0, 0.0).astype(BF16)

    def place(i, s):
        safe = jnp.maximum(slots[s, 0, i], 0)
        rest, qz = split(safe, layers_z)
        qx, qy = split(rest, columns_y)
        half, layer = split(qz, 16)
        first = 8 + qx * (4 * size_y) + qy * 4
        return half, first, 8 * layer

    def windows(half, first, c):
        return [
            (half, pl.ds(first + ((c * size_x + ax) * size_y - 4 * (ax % 2)), 8)) for ax in range(4)
        ]

    def gather(i, g):
        for s in range(count_s):
            half, first, shift = place(i, s)
            for c in range(3):
                w = [field[k, at, :] for k, at in windows(half, first, c)]
                near = pltpu.roll(jnp.where(low_sub, w[0], w[1]), (128 - shift) & 127, 1)
                far = pltpu.roll(jnp.where(low_sub, w[2], w[3]), (192 - shift) & 127, 1)
                stage[pl.ds(((g * count_s + s) * 8 + c) * 8, 8), :] = jnp.where(low_lane, near, far)

    slot_of = lax.broadcasted_iota(jnp.int32, (8, width), 1) // markers

    def force_and_spread(i, g):
        block_w = blocks[i, 0:width, :]
        tail = blocks[i, width : width + 16, :].astype(F32)
        target = jnp.concatenate([tail[0:8, :], tail[8:16, 0 : width - 128]], axis=1)
        mine = pl.ds(pl.multiple_of(i * (count_s * 8), 8), count_s * 8)
        product = lax.dot_general(
            chosen[mine, :].astype(BF16), block_w, (((1,), (1,)), ((), ())), preferred_element_type=F32
        )
        interp = product[0:8]
        live = jnp.full((8, width), slots[0, 0, i], jnp.int32)
        for s in range(1, count_s):
            interp = jnp.where(slot_of == s, product[8 * s : 8 * s + 8], interp)
            live = jnp.where(slot_of == s, slots[s, 0, i], live)
        force = jnp.where(live >= 0, (target - interp) / time_step, 0.0)
        force_out[i] = force[0:3, :]
        rows = jnp.concatenate([jnp.where(slot_of == s, force, 0.0) for s in range(count_s)], axis=0)
        chosen[mine, :] = jnp.dot(rows.astype(BF16), block_w, preferred_element_type=F32)

    def scatter(i, g):
        for s in range(count_s):
            half, first, shift = place(i, s)
            for c in range(3):
                both = stage[pl.ds(((g * count_s + s) * 8 + c) * 8, 8), :]
                near = pltpu.roll(jnp.where(low_lane, both, 0.0), shift, 1)
                far = pltpu.roll(jnp.where(low_lane, 0.0, both), (shift + 64) & 127, 1)
                spots = windows(half, first, c)
                pieces = [near, near, far, far]
                sums = [
                    field[k, at, :] + jnp.where(low_sub, *((pieces[ax], 0.0) if ax % 2 == 0 else (0.0, pieces[ax])))
                    for ax, (k, at) in enumerate(spots)
                ]
                for (k, at), total in zip(spots, sums):
                    field[k, at, :] = total

    def first_pass(k):
        for g in range(group):
            gather(k * group + g, g)
        picked = jnp.concatenate([stage[pl.ds(r, lines, stride=8), :] for r in range(8)], axis=1)
        picked = jnp.dot(picked.astype(BF16), shifts(1024, 128, 0), preferred_element_type=F32)
        chosen[pl.ds(pl.multiple_of(k * lines, 8), lines), :] = picked
        for g in range(group):
            force_and_spread(k * group + g, g)

    def second_pass(k):
        rows = chosen[pl.ds(pl.multiple_of(k * lines, 8), lines), :] * (time_step * spread_gain)
        high = rows.astype(BF16)
        pair = jnp.concatenate([high, (rows - high.astype(F32)).astype(BF16)], axis=1)
        pieces = jnp.dot(pair, shifts(256, 1024, 1), preferred_element_type=F32)
        for r in range(8):
            stage[pl.ds(r, lines, stride=8), :] = pieces[:, r * 128 : r * 128 + 128]
        for g in range(group):
            scatter(k * group + g, g)

    each(count_d // group, first_pass)
    each(count_d // group, second_pass)
    for part in range(halves):
        out[:, part * 128 : part * 128 + 128] = field[part, pl.ds(8, cells), :]


def run_main(dims, *operands):
    size_x, size_y, size_z, count_d, count_s, width = dims
    cells = 3 * size_x * size_y
    group = 8 if count_d % 8 == 0 else 1
    inside = pl.BlockSpec(memory_space=VMEM)
    return pl.pallas_call(
        functools.partial(main_kernel, dims),
        out_shape=(
            jax.ShapeDtypeStruct((cells, size_z), F32),
            jax.ShapeDtypeStruct((count_d, 3, width), F32),
        ),
        in_specs=[pl.BlockSpec(memory_space=pltpu.SMEM)] + [inside] * 6,
        out_specs=(inside, inside),
        scratch_shapes=[
            VMEM((size_z // 128, cells + 16, 128), F32),
            VMEM((group * count_s * 64, 128), F32),
            VMEM((count_d * count_s * 8, 128), F32),
        ],
        compiler_params=pltpu.CompilerParams(vmem_limit_bytes=24 * 2**20),
        name="main",
    )(*operands)


def shards(velocity, weights, targets, owner_list, slot_patch):
    size_x, size_y, size_z = velocity.shape[1:]
    count_d, count_s, markers = weights.shape[2:5]
    width = count_s * markers
    cells = 3 * size_x * size_y
    vel = velocity.reshape(cells, size_z)
    block_w = weights.reshape(count_d, width, 128)
    anywhere = pl.BlockSpec(memory_space=pl.ANY)
    inside = pl.BlockSpec(memory_space=VMEM)
    face_x = jax.ShapeDtypeStruct((3, size_y, size_z), F32)
    face_y = jax.ShapeDtypeStruct((3, size_x, size_z), F32)
    chunk, x_first, x_last, y_first, y_last = pl.pallas_call(
        functools.partial(pack_kernel, (size_x, size_y, count_d, width)),
        out_shape=(
            jax.ShapeDtypeStruct((count_d, width + 16, 128), BF16),
            face_x, face_x, face_y, face_y,
        ),
        in_specs=[anywhere, anywhere, inside],
        out_specs=(inside,) * 5,
        scratch_shapes=[
            VMEM((size_z // 128, cells, 128), F32),
            VMEM((count_d * 16, 128), F32),
            pltpu.SemaphoreType.DMA((1 + size_z // 128,)),
        ],
        compiler_params=pltpu.CompilerParams(vmem_limit_bytes=56 * 2**20),
        name="pack",
    )(vel, block_w, jnp.transpose(targets[0, 0], (1, 0, 2)))

    def ring(x, axis, step):
        size = lax.axis_size(axis)
        return lax.ppermute(x, axis, [(i, (i + step) % size) for i in range(size)])

    y_before = ring(y_last, "gy", 1)
    y_after = ring(y_first, "gy", -1)
    x_before = ring(x_last, "gx", 1)
    x_after = ring(x_first, "gx", -1)
    arrived = lax.all_to_all(chunk, "gx", split_axis=0, concat_axis=0, tiled=True)
    slots = jnp.transpose(slot_patch[0, 0]).reshape(count_s, 1, count_d)
    dims = (size_x, size_y, size_z, count_d, count_s, width)
    out, force = run_main(dims, slots, vel, x_before, x_after, y_before, y_after, arrived)
    returned = lax.all_to_all(force, "gx", split_axis=0, concat_axis=0, tiled=True)
    return out.reshape(velocity.shape), returned[None, None]


def solution(mesh):
    return jax.shard_map(
        shards,
        mesh=mesh,
        in_specs=(
            P(None, "gx", "gy", None),
            P("gx", "gy", None, None, None, None),
            P("gx", "gy", None, None, None),
            P("gx", "gy", None, None),
            P("gx", "gy", None, None),
        ),
        out_specs=(P(None, "gx", "gy", None), P("gx", "gy", None, None, None)),
        check_vma=False,
    )
```

```python
import functools

import jax
import jax.numpy as jnp
from jax import lax
from jax.experimental import pallas as pl
from jax.experimental.pallas import tpu as pltpu
from jax.sharding import PartitionSpec as P

time_step = 0.05
viscosity = 0.5
spread_gain = 0.5

VMEM = pltpu.VMEM
F32 = jnp.float32
BF16 = jnp.bfloat16


def each(count, body, flat=False):
    if flat or count == 1:
        for i in range(count):
            body(i)
    else:

        def step(i, carry):
            body(i)
            return carry

        lax.fori_loop(0, count, step, 0)


def faces_kernel(dims, vel, x_first, x_last, y_first, y_last, held, sems):
    size_x, size_y = dims
    halves = held.shape[0]
    moves = [
        pltpu.make_async_copy(vel.at[:, pl.ds(part * 128, 128)], held.at[part], sems.at[part])
        for part in range(halves)
    ]
    for move in moves:
        move.start()
    plane = size_x * size_y
    for part in range(halves):
        moves[part].wait()
        lanes = pl.ds(part * 128, 128)
        for c in range(3):
            x_first[c, :, lanes] = held[part, pl.ds(c * plane, size_y), :]
            x_last[c, :, lanes] = held[part, pl.ds(c * plane + plane - size_y, size_y), :]
            y_first[c, :, lanes] = held[part, pl.ds(c * plane, size_x, stride=size_y), :]
            y_last[c, :, lanes] = held[part, pl.ds(c * plane + size_y - 1, size_x, stride=size_y), :]


def pack_kernel(dims, w, t, slots, own, chunk, slots_out, own_out, rows, sem):
    slots_out[...] = slots[...]
    own_out[...] = own[...]
    count_d, width = dims
    move_w = pltpu.make_async_copy(w, chunk.at[:, pl.ds(0, width), :], sem)
    move_w.start()
    rows[...] = jnp.zeros_like(rows)
    rest = jnp.zeros((count_d, 256 - width), F32)
    for c in range(3):
        values = t[c].astype(F32)
        rows[pl.ds(c, count_d, stride=16), :] = values[:, 0:128]
        rows[pl.ds(8 + c, count_d, stride=16), :] = jnp.concatenate([values[:, 128:width], rest], axis=1)
    chunk[:, width : width + 16, :] = rows[...].astype(BF16).reshape(count_d, 16, 128)
    move_w.wait()


def split(x, size):
    if size & (size - 1) == 0:
        return lax.shift_right_logical(x, size.bit_length() - 1), x & (size - 1)
    return lax.div(x, size), lax.rem(x, size)


def shifts(rows, columns, piece_axis):
    shape = (rows, columns)
    piece = lax.broadcasted_iota(jnp.int32, shape, piece_axis)
    place = lax.broadcasted_iota(jnp.int32, shape, 1 - piece_axis) & 127
    m = piece & 127
    hit = ((m & 63) < 8) & (place == m + 8 * lax.shift_right_logical(piece, 7))
    return jnp.where(hit, 1.0, 0.0).astype(BF16)


def locate(dims, slots, i, s):
    size_x, size_y, size_z = dims[:3]
    safe = jnp.maximum(slots[0, s, 0, i], 0)
    rest, qz = split(safe, size_z // 8)
    qx, qy = split(rest, size_y // 4)
    half, layer = split(qz, 16)
    first = 8 + qx * (4 * size_y) + qy * 4
    return half, first, 8 * layer


def windows(dims, half, first, c):
    size_x, size_y = dims[:2]
    return [(half, pl.ds(first + ((c * size_x + ax) * size_y - 4 * (ax % 2)), 8)) for ax in range(4)]


def low_halves():
    lane = lax.broadcasted_iota(jnp.int32, (8, 128), 1)
    sub = lax.broadcasted_iota(jnp.int32, (8, 128), 0)
    return lane < 64, sub < 4


def select_slots(product, slot_of, count_s):
    interp = product[0:8]
    for s in range(1, count_s):
        interp = jnp.where(slot_of == s, product[8 * s : 8 * s + 8], interp)
    return interp


def predict_kernel(
    dims, slots, me_ref, vel, x_before, x_after, y_before, y_after, field, keep, give, stage,
):
    size_x, size_y, size_z, count_d, count_s, width = dims
    halves = size_z // 128
    me = me_ref[0]

    row = lax.broadcasted_iota(jnp.int32, (size_y, size_z), 0)
    col = lax.broadcasted_iota(jnp.int32, (size_y, size_z), 1)

    def stencil(x):
        center, fore, back, right, left, top, bottom = [], [], [], [], [], [], []
        for c in range(3):
            base = (c * size_x + x) * size_y
            here = vel[pl.ds(base, size_y), :]
            center.append(here)
            fore.append(x_after[c] if x == size_x - 1 else vel[pl.ds(base + size_y, size_y), :])
            back.append(x_before[c] if x == 0 else vel[pl.ds(base - size_y, size_y), :])
            right.append(
                jnp.where(row == size_y - 1, y_after[c, pl.ds(x, 1), :], pltpu.roll(here, size_y - 1, 0))
            )
            left.append(jnp.where(row == 0, y_before[c, pl.ds(x, 1), :], pltpu.roll(here, 1, 0)))
            top.append(jnp.where(col == size_z - 1, 0.0, pltpu.roll(here, size_z - 1, 1)))
            bottom.append(jnp.where(col == 0, 0.0, pltpu.roll(here, 1, 1)))
        for c in range(3):
            laplace = fore[c] + back[c] + right[c] + left[c] + top[c] + bottom[c] - 6.0 * center[c]
            advect = (
                center[0] * (fore[c] - back[c]) * 0.5
                + center[1] * (right[c] - left[c]) * 0.5
                + center[2] * (top[c] - bottom[c]) * 0.5
            )
            base = 8 + (c * size_x + x) * size_y
            result = center[c] + time_step * (viscosity * laplace - advect)
            for part in range(halves):
                field[part, pl.ds(base, size_y), :] = result[:, part * 128 : part * 128 + 128]

    each(size_x, stencil, True)

    low_lane, low_sub = low_halves()
    group = 8 if count_d % 8 == 0 else count_d
    lines = group * count_s * 8
    tail = jnp.zeros((keep.shape[1] - count_s * 8, 128), F32)

    def gather(i, g):
        for s in range(count_s):
            half, first, shift = locate(dims, slots, i, s)
            for c in range(3):
                w = [field[k, at, :] for k, at in windows(dims, half, first, c)]
                near = pltpu.roll(jnp.where(low_sub, w[0], w[1]), (128 - shift) & 127, 1)
                far = pltpu.roll(jnp.where(low_sub, w[2], w[3]), (192 - shift) & 127, 1)
                stage[pl.ds(((g * count_s + s) * 8 + c) * 8, 8), :] = jnp.where(low_lane, near, far)

    def batch(k):
        for g in range(group):
            gather(me ^ (k * group + g), g)
        picked = jnp.concatenate([stage[pl.ds(r, lines, stride=8), :] for r in range(8)], axis=1)
        picked = jnp.dot(picked.astype(BF16), shifts(1024, 128, 0), preferred_element_type=F32)
        for g in range(group):
            mine = picked[g * count_s * 8 : (g + 1) * count_s * 8]
            block = jnp.concatenate([mine, tail], axis=0).astype(BF16)
            (give if g % 2 else keep)[k * (group // 2) + g // 2] = block

    each(count_d // group, batch)


def spread_kernel(dims, slots, me_ref, before, keep, give, blocks, out, token, field, stage, chosen):
    size_x, size_y, size_z, count_d, count_s, width = dims
    cells = 3 * size_x * size_y
    halves = size_z // 128
    me = me_ref[0]
    low_lane, low_sub = low_halves()
    group = 8 if count_d % 8 == 0 else count_d
    lines = group * count_s * 8
    slot_of = lax.broadcasted_iota(jnp.int32, (8, width), 1) // (width // count_s)
    field[...] = before[...]
    token[...] = jnp.zeros_like(token)

    def force(i, g, block):
        block_w = blocks[i, 0:width, :]
        tail = blocks[i, width : width + 16, :].astype(F32)
        target = jnp.concatenate([tail[0:8, :], tail[8:16, 0 : width - 128]], axis=1)
        product = lax.dot_general(
            block, block_w, (((1,), (1,)), ((), ())), preferred_element_type=F32
        )
        interp = select_slots(product, slot_of, count_s)
        live = jnp.full((8, width), slots[0, 0, 0, i], jnp.int32)
        for s in range(1, count_s):
            live = jnp.where(slot_of == s, slots[0, s, 0, i], live)
        value = jnp.where(live >= 0, (target - interp) / time_step, 0.0)
        rows = jnp.concatenate([jnp.where(slot_of == s, value, 0.0) for s in range(count_s)], axis=0)
        chosen[pl.ds(g * count_s * 8, count_s * 8), :] = jnp.dot(
            rows.astype(BF16), block_w, preferred_element_type=F32
        )

    def scatter(i, g):
        for s in range(count_s):
            half, first, shift = locate(dims, slots, i, s)
            for c in range(3):
                both = stage[pl.ds(((g * count_s + s) * 8 + c) * 8, 8), :]
                near = pltpu.roll(jnp.where(low_lane, both, 0.0), shift, 1)
                far = pltpu.roll(jnp.where(low_lane, 0.0, both), (shift + 64) & 127, 1)
                spots = windows(dims, half, first, c)
                pieces = [
                    jnp.where(low_sub, near, 0.0), jnp.where(low_sub, 0.0, near),
                    jnp.where(low_sub, far, 0.0), jnp.where(low_sub, 0.0, far),
                ]
                sums = [field[k, at, :] + piece for (k, at), piece in zip(spots, pieces)]
                for (k, at), total in zip(spots, sums):
                    field[k, at, :] = total

    def batch(k):
        for g in range(group):
            block = (give if g % 2 else keep)[k * (group // 2) + g // 2]
            force(me ^ (k * group + g), g, block)
        rows = chosen[...] * (time_step * spread_gain)
        high = rows.astype(BF16)
        pair = jnp.concatenate([high, (rows - high.astype(F32)).astype(BF16)], axis=1)
        pieces = jnp.dot(pair, shifts(256, 1024, 1), preferred_element_type=F32)
        for r in range(8):
            stage[pl.ds(r, lines, stride=8), :] = pieces[:, r * 128 : r * 128 + 128]
        for g in range(group):
            scatter(me ^ (k * group + g), g)

    each(count_d // group, batch)
    for part in range(halves):
        out[:, part * 128 : part * 128 + 128] = field[part, pl.ds(8, cells), :]


def owner_kernel(dims, slots, me_ref, token, targets, block_w, keep, first, *rest):
    size_x, size_y, size_z, count_d, count_s, width = dims
    received, out, picked = rest[:-2], rest[-2], rest[-1]
    me = me_ref[0]
    group = 8 if count_d % 8 == 0 else count_d
    slot_of = lax.broadcasted_iota(jnp.int32, (8, width), 1) // (width // count_s)
    row = lax.broadcasted_iota(jnp.int32, (group, width), 0)
    column_slot = lax.broadcasted_iota(jnp.int32, (group, width), 1) // (width // count_s)
    picked[0] = keep[0]
    picked[1] = first[0]
    for k, pair in enumerate(received):
        picked[2 * k + 2] = pair[0]
        picked[2 * k + 3] = pair[1]

    def batch(k):
        interp = [jnp.zeros((group, width), F32) for c in range(3)]
        live = jnp.full((group, width), -1, jnp.int32)
        for g in range(group):
            d = k * group + g
            product = lax.dot_general(
                picked[me ^ d], block_w[d], (((1,), (1,)), ((), ())), preferred_element_type=F32
            )
            lines = select_slots(product, slot_of, count_s)
            for c in range(3):
                interp[c] = jnp.where(row == g, lines[c : c + 1], interp[c])
            for s in range(count_s):
                live = jnp.where((row == g) & (column_slot == s), slots[0, s, 0, d], live)
        for c in range(3):
            at = pl.ds(k * group, group)
            target = targets[c, at, :].astype(F32)
            out[c, at, :] = jnp.where(live >= 0, (target - interp[c]) / time_step, 0.0)

    each(count_d // group, batch)


def shards(velocity, weights, targets, owner_list, slot_patch):
    size_x, size_y, size_z = velocity.shape[1:]
    count_d, count_s, markers = weights.shape[2:5]
    width = count_s * markers
    cells = 3 * size_x * size_y
    vel = velocity.reshape(cells, size_z)
    block_w = weights.reshape(count_d, width, 128)
    wanted = jnp.transpose(targets[0, 0], (1, 0, 2))
    slots = jnp.transpose(slot_patch, (0, 3, 1, 2))
    own = jnp.transpose(owner_list, (0, 3, 1, 2))
    me = jnp.full((1,), lax.axis_index("gx"), jnp.int32)
    dims = (size_x, size_y, size_z, count_d, count_s, width)
    group = 8 if count_d % 8 == 0 else count_d
    high = -(-count_s * 8 // 16) * 16
    anywhere = pl.BlockSpec(memory_space=pl.ANY)
    inside = pl.BlockSpec(memory_space=VMEM)
    scalars = pl.BlockSpec(memory_space=pltpu.SMEM)
    face_x = jax.ShapeDtypeStruct((3, size_y, size_z), F32)
    face_y = jax.ShapeDtypeStruct((3, size_x, size_z), F32)
    half = jax.ShapeDtypeStruct((count_d // 2, high, 128), BF16)
    padded = (size_z // 128, cells + 16, 128)
    params = pltpu.CompilerParams(vmem_limit_bytes=24 * 2**20)
    table = jax.ShapeDtypeStruct(slots.shape, jnp.int32)
    x_first, x_last, y_first, y_last = pl.pallas_call(
        functools.partial(faces_kernel, (size_x, size_y)),
        out_shape=(face_x, face_x, face_y, face_y),
        in_specs=[anywhere],
        out_specs=(inside,) * 4,
        scratch_shapes=[
            VMEM((size_z // 128, cells, 128), F32),
            pltpu.SemaphoreType.DMA((size_z // 128,)),
        ],
        compiler_params=pltpu.CompilerParams(vmem_limit_bytes=24 * 2**20),
        name="faces",
    )(vel)
    chunk, slots, own = pl.pallas_call(
        functools.partial(pack_kernel, (count_d, width)),
        out_shape=(jax.ShapeDtypeStruct((count_d, width + 16, 128), BF16), table, table),
        in_specs=[anywhere, inside, inside, inside],
        out_specs=(inside,) * 3,
        scratch_shapes=[VMEM((count_d * 16, 128), F32), pltpu.SemaphoreType.DMA],
        compiler_params=params,
        name="pack",
    )(block_w, wanted, slots, own)

    def ring(x, axis, step):
        size = lax.axis_size(axis)
        return lax.ppermute(x, axis, [(i, (i + step) % size) for i in range(size)])

    def swap(x, mask):
        return lax.ppermute(x, "gx", [(i, i ^ mask) for i in range(lax.axis_size("gx"))])

    x_before = ring(x_last, "gx", 1)
    x_after = ring(x_first, "gx", -1)
    y_before = ring(y_last, "gy", 1)
    y_after = ring(y_first, "gy", -1)
    arrived = lax.all_to_all(chunk, "gx", split_axis=0, concat_axis=0, tiled=True)
    field, keep, give = pl.pallas_call(
        functools.partial(predict_kernel, dims),
        out_shape=(jax.ShapeDtypeStruct(padded, F32), half, half),
        in_specs=[scalars, scalars] + [inside] * 5,
        out_specs=(inside,) * 3,
        scratch_shapes=[VMEM((group * count_s * 64, 128), F32)],
        compiler_params=params,
        name="predict",
    )(slots, me, vel, x_before, x_after, y_before, y_after)
    first = swap(give, 1)
    received = [swap(jnp.stack([keep[k], first[k]]), 2 * k) for k in range(1, count_d // 2)]
    out, token = pl.pallas_call(
        functools.partial(spread_kernel, dims),
        out_shape=(jax.ShapeDtypeStruct((cells, size_z), F32), jax.ShapeDtypeStruct((8, 128), F32)),
        in_specs=[scalars, scalars] + [inside] * 4,
        out_specs=(inside, inside),
        scratch_shapes=[
            VMEM(padded, F32),
            VMEM((group * count_s * 64, 128), F32),
            VMEM((group * count_s * 8, 128), F32),
        ],
        compiler_params=params,
        cost_estimate=pl.CostEstimate(flops=10**8, bytes_accessed=4 * 10**6, transcendentals=0),
        name="spread",
    )(slots, me, field, keep, give, arrived)
    force = pl.pallas_call(
        functools.partial(owner_kernel, dims),
        out_shape=jax.ShapeDtypeStruct((3, count_d, width), F32),
        in_specs=[scalars, scalars] + [inside] * (4 + count_d // 2),
        out_specs=inside,
        scratch_shapes=[VMEM((count_d, high, 128), BF16)],
        compiler_params=params,
        name="owner",
    )(own, me, token, wanted, block_w, keep, first, *received)
    return out.reshape(velocity.shape), jnp.transpose(force, (1, 0, 2))[None, None]


def solution(mesh):
    return jax.shard_map(
        shards,
        mesh=mesh,
        in_specs=(
            P(None, "gx", "gy", None),
            P("gx", "gy", None, None, None, None),
            P("gx", "gy", None, None, None),
            P("gx", "gy", None, None),
            P("gx", "gy", None, None),
        ),
        out_specs=(P(None, "gx", "gy", None), P("gx", "gy", None, None, None)),
        check_vma=False,
    )
```

```python
import functools

import jax
import jax.numpy as jnp
import ml_dtypes
import numpy as np
from jax import lax
from jax.experimental import pallas as pl
from jax.experimental.pallas import tpu as pltpu
from jax.sharding import PartitionSpec as P

time_step = 0.05
viscosity = 0.5
spread_gain = 0.5

VMEM = pltpu.VMEM
F32 = jnp.float32
BF16 = jnp.bfloat16


def each(count, body, flat=False):
    if flat or count == 1:
        for i in range(count):
            body(i)
    else:

        def step(i, carry):
            body(i)
            return carry

        lax.fori_loop(0, count, step, 0)


def faces_kernel(dims, vel, x_first, x_last, y_first, y_last, held, sems):
    size_x, size_y = dims
    halves = held.shape[0]
    moves = [
        pltpu.make_async_copy(vel.at[:, pl.ds(part * 128, 128)], held.at[part], sems.at[part])
        for part in range(halves)
    ]
    for move in moves:
        move.start()
    plane = size_x * size_y
    for part in range(halves):
        moves[part].wait()
        lanes = pl.ds(part * 128, 128)
        for c in range(3):
            x_first[c, :, lanes] = held[part, pl.ds(c * plane, size_y), :]
            x_last[c, :, lanes] = held[part, pl.ds(c * plane + plane - size_y, size_y), :]
            y_first[c, :, lanes] = held[part, pl.ds(c * plane, size_x, stride=size_y), :]
            y_last[c, :, lanes] = held[part, pl.ds(c * plane + size_y - 1, size_x, stride=size_y), :]


def pack_kernel(dims, w, t, slots, own, chunk, slots_out, own_out, rows, sem):
    slots_out[...] = slots[...]
    own_out[...] = own[...]
    count_d, width = dims
    move_w = pltpu.make_async_copy(w, chunk.at[:, pl.ds(0, width), :], sem)
    move_w.start()
    rows[...] = jnp.zeros_like(rows)
    rest = jnp.zeros((count_d, 256 - width), F32)
    for c in range(3):
        values = t[c].astype(F32)
        rows[pl.ds(c, count_d, stride=16), :] = values[:, 0:128]
        rows[pl.ds(8 + c, count_d, stride=16), :] = jnp.concatenate([values[:, 128:width], rest], axis=1)
    chunk[:, width : width + 16, :] = rows[...].astype(BF16).reshape(count_d, 16, 128)
    move_w.wait()


def split(x, size):
    if size & (size - 1) == 0:
        return lax.shift_right_logical(x, size.bit_length() - 1), x & (size - 1)
    return lax.div(x, size), lax.rem(x, size)


def shifts():
    piece = np.arange(1024)[:, None]
    m = piece % 128
    hit = (m % 64 < 8) & (np.arange(128)[None, :] == m + 8 * (piece // 128))
    return hit.astype(ml_dtypes.bfloat16)


def locate(dims, slots, i, s):
    size_x, size_y, size_z = dims[:3]
    safe = jnp.maximum(slots[0, s, 0, i], 0)
    rest, qz = split(safe, size_z // 8)
    qx, qy = split(rest, size_y // 4)
    half, layer = split(qz, 16)
    first = 8 + qx * (4 * size_y) + qy * 4
    return half, first, 8 * layer


def windows(dims, half, first, c):
    size_x, size_y = dims[:2]
    return [(half, pl.ds(first + ((c * size_x + ax) * size_y - 4 * (ax % 2)), 8)) for ax in range(4)]


def low_halves():
    lane = lax.broadcasted_iota(jnp.int32, (8, 128), 1)
    sub = lax.broadcasted_iota(jnp.int32, (8, 128), 0)
    return lane < 64, sub < 4


def select_slots(product, slot_of, count_s):
    interp = None
    for s in range(count_s):
        part = product[s // 2 * 8 : s // 2 * 8 + 8]
        if s % 2:
            part = pltpu.roll(part, 4, 0)
        interp = part if s == 0 else jnp.where(slot_of == s, part, interp)
    return interp


def predict_kernel(
    dims, table, vel, x_before, x_after, y_before, y_after, gathers, field, keep, give, stage, slots, sem,
):
    size_x, size_y, size_z, count_d, count_s, width = dims
    halves = size_z // 128
    me = lax.axis_index("gx")
    move = pltpu.make_async_copy(table, slots, sem)
    move.start()

    row = lax.broadcasted_iota(jnp.int32, (size_y, size_z), 0)
    col = lax.broadcasted_iota(jnp.int32, (size_y, size_z), 1)

    def stencil(x):
        center, fore, back, right, left, top, bottom = [], [], [], [], [], [], []
        for c in range(3):
            base = (c * size_x + x) * size_y
            here = vel[pl.ds(base, size_y), :]
            center.append(here)
            fore.append(x_after[c] if x == size_x - 1 else vel[pl.ds(base + size_y, size_y), :])
            back.append(x_before[c] if x == 0 else vel[pl.ds(base - size_y, size_y), :])
            right.append(
                jnp.where(row == size_y - 1, y_after[c, pl.ds(x, 1), :], pltpu.roll(here, size_y - 1, 0))
            )
            left.append(jnp.where(row == 0, y_before[c, pl.ds(x, 1), :], pltpu.roll(here, 1, 0)))
            top.append(jnp.where(col == size_z - 1, 0.0, pltpu.roll(here, size_z - 1, 1)))
            bottom.append(jnp.where(col == 0, 0.0, pltpu.roll(here, 1, 1)))
        for c in range(3):
            total = (
                (fore[c] + back[c]) - center[0] * (fore[c] - back[c])
                + (right[c] + left[c]) - center[1] * (right[c] - left[c])
                + (top[c] + bottom[c]) - center[2] * (top[c] - bottom[c])
            )
            base = 8 + (c * size_x + x) * size_y
            result = (1.0 - 6.0 * time_step * viscosity) * center[c] + (0.5 * time_step) * total
            for part in range(halves):
                field[part, pl.ds(base, size_y), :] = result[:, part * 128 : part * 128 + 128]

    each(size_x, stencil, True)

    move.wait()
    low_lane, low_sub = low_halves()
    group = 8 if count_d % 8 == 0 else count_d
    high = keep.shape[1]
    lines = group * high

    def gather(i, g):
        for s in range(count_s):
            half, first, shift = locate(dims, slots, i, s)
            for c in range(3):
                w = [field[k, at, :] for k, at in windows(dims, half, first, c)]
                near = pltpu.roll(jnp.where(low_sub, w[0], w[1]), (128 - shift) & 127, 1)
                far = pltpu.roll(jnp.where(low_sub, w[2], w[3]), (192 - shift) & 127, 1)
                stage[pl.ds((g * high + s * 4 + c) * 8, 8), :] = jnp.where(low_lane, near, far)

    def batch(k):
        for g in range(group):
            gather(me ^ (k * group + g), g)
        picked = jnp.concatenate([stage[pl.ds(r, lines, stride=8), :] for r in range(8)], axis=1)
        picked = jnp.dot(picked.astype(BF16), gathers[...], preferred_element_type=F32).astype(BF16)
        for g in range(group):
            (give if g % 2 else keep)[k * (group // 2) + g // 2] = picked[g * high : (g + 1) * high]

    stage[...] = jnp.zeros_like(stage)
    each(count_d // group, batch)


def spread_kernel(
    dims, table, before, keep, give, blocks, scatters, out, token, field, stage, chosen, slots, sems,
):
    size_x, size_y, size_z, count_d, count_s, width = dims
    cells = 3 * size_x * size_y
    halves = size_z // 128
    me = lax.axis_index("gx")
    move_field = pltpu.make_async_copy(before, field, sems.at[0])
    move_slots = pltpu.make_async_copy(table, slots, sems.at[1])
    move_slots.start()
    move_field.start()
    token[...] = jnp.zeros_like(token)
    low_lane, low_sub = low_halves()
    group = 8 if count_d % 8 == 0 else count_d
    high = keep.shape[1]
    lines = group * high
    slot_of = lax.broadcasted_iota(jnp.int32, (8, width), 1) // (width // count_s)
    low_row = lax.broadcasted_iota(jnp.int32, (8, width), 0) < 4

    def interpolate(i, block):
        return lax.dot_general(
            block, blocks[i, 0:width, :], (((1,), (1,)), ((), ())), preferred_element_type=F32
        )

    def force(i, product):
        tail = blocks[i, width : width + 16, :].astype(F32)
        target = jnp.concatenate([tail[0:8, :], tail[8:16, 0 : width - 128]], axis=1)
        interp = select_slots(product, slot_of, count_s)
        live = jnp.full((8, width), slots[0, 0, 0, i], jnp.int32)
        for s in range(1, count_s):
            live = jnp.where(slot_of == s, slots[0, s, 0, i], live)
        value = jnp.where(live >= 0, (target - interp) / time_step, 0.0)
        swapped = pltpu.roll(value, 4, 0)
        rows = []
        for first in range(0, high // 4, 2):
            lower = jnp.where(slot_of == first, value, 0.0)
            upper = jnp.where(slot_of == first + 1, swapped, 0.0)
            rows.append(jnp.where(low_row, lower, upper))
        return jnp.concatenate(rows, axis=0).astype(BF16)

    def scatter(i, g):
        for s in range(count_s):
            half, first, shift = locate(dims, slots, i, s)
            for c in range(3):
                both = stage[pl.ds((g * high + s * 4 + c) * 8, 8), :]
                near = pltpu.roll(jnp.where(low_lane, both, 0.0), shift, 1)
                far = pltpu.roll(jnp.where(low_lane, 0.0, both), (shift + 64) & 127, 1)
                spots = windows(dims, half, first, c)
                pieces = [
                    jnp.where(low_sub, near, 0.0), jnp.where(low_sub, 0.0, near),
                    jnp.where(low_sub, far, 0.0), jnp.where(low_sub, 0.0, far),
                ]
                sums = [field[k, at, :] + piece for (k, at), piece in zip(spots, pieces)]
                for (k, at), total in zip(spots, sums):
                    field[k, at, :] = total

    def batch(k):
        owners = [me ^ (k * group + g) for g in range(group)]
        products = [
            interpolate(owners[g], (give if g % 2 else keep)[k * (group // 2) + g // 2])
            for g in range(group)
        ]
        if count_d == group:
            move_slots.wait()
        forces = [force(owners[g], products[g]) for g in range(group)]
        for g in range(group):
            chosen[pl.ds(g * high, high), :] = jnp.dot(
                forces[g], blocks[owners[g], 0:width, :], preferred_element_type=F32
            )
        rows = chosen[...] * (time_step * spread_gain)
        upper = rows.astype(BF16)
        lower = (rows - upper.astype(F32)).astype(BF16)
        pieces = jnp.dot(upper, scatters[...], preferred_element_type=F32)
        pieces = pieces + jnp.dot(lower, scatters[...], preferred_element_type=F32)
        for r in range(8):
            stage[pl.ds(r, lines, stride=8), :] = pieces[:, r * 128 : r * 128 + 128]
        if count_d == group:
            move_field.wait()
        for g in range(group):
            scatter(owners[g], g)

    if count_d != group:
        move_slots.wait()
        move_field.wait()
    each(count_d // group, batch)
    moves = [
        pltpu.make_async_copy(
            field.at[part, pl.ds(8, cells), :], out.at[:, pl.ds(part * 128, 128)], sems.at[2 + part]
        )
        for part in range(halves)
    ]
    for move in moves:
        move.start()
    for move in moves:
        move.wait()


def owner_kernel(dims, table, token, targets, block_w, keep, first, *rest):
    size_x, size_y, size_z, count_d, count_s, width = dims
    received, (out, picked, slots, sem) = rest[:-4], rest[-4:]
    me = lax.axis_index("gx")
    move = pltpu.make_async_copy(table, slots, sem)
    move.start()
    group = 8 if count_d % 8 == 0 else count_d
    slot_of = lax.broadcasted_iota(jnp.int32, (8, width), 1) // (width // count_s)
    row = lax.broadcasted_iota(jnp.int32, (group, width), 0)
    column_slot = lax.broadcasted_iota(jnp.int32, (group, width), 1) // (width // count_s)
    picked[0] = keep[0]
    picked[1] = first[0]
    for k, pair in enumerate(received):
        picked[2 * k + 2] = pair[0]
        picked[2 * k + 3] = pair[1]
    if count_d != group:
        move.wait()

    def batch(k):
        products = [
            lax.dot_general(
                picked[me ^ (k * group + g)], block_w[k * group + g],
                (((1,), (1,)), ((), ())), preferred_element_type=F32,
            )
            for g in range(group)
        ]
        if count_d == group:
            move.wait()
        interp = [jnp.zeros((group, width), F32) for c in range(3)]
        live = jnp.full((group, width), -1, jnp.int32)
        for g in range(group):
            lines = select_slots(products[g], slot_of, count_s)
            for c in range(3):
                interp[c] = jnp.where(row == g, lines[c : c + 1], interp[c])
            for s in range(count_s):
                live = jnp.where((row == g) & (column_slot == s), slots[0, s, 0, k * group + g], live)
        for c in range(3):
            at = pl.ds(k * group, group)
            target = targets[c, at, :].astype(F32)
            out[c, at, :] = jnp.where(live >= 0, (target - interp[c]) / time_step, 0.0)

    each(count_d // group, batch)


def shards(velocity, weights, targets, owner_list, slot_patch):
    size_x, size_y, size_z = velocity.shape[1:]
    count_d, count_s, markers = weights.shape[2:5]
    width = count_s * markers
    cells = 3 * size_x * size_y
    vel = velocity.reshape(cells, size_z)
    block_w = weights.reshape(count_d, width, 128)
    wanted = jnp.transpose(targets[0, 0], (1, 0, 2))
    slots = jnp.transpose(slot_patch, (0, 3, 1, 2))
    own = jnp.transpose(owner_list, (0, 3, 1, 2))
    dims = (size_x, size_y, size_z, count_d, count_s, width)
    group = 8 if count_d % 8 == 0 else count_d
    high = -(-count_s * 4 // 16) * 16
    anywhere = pl.BlockSpec(memory_space=pl.ANY)
    inside = pl.BlockSpec(memory_space=VMEM)
    face_x = jax.ShapeDtypeStruct((3, size_y, size_z), F32)
    face_y = jax.ShapeDtypeStruct((3, size_x, size_z), F32)
    half = jax.ShapeDtypeStruct((count_d // 2, high, 128), BF16)
    padded = (size_z // 128, cells + 16, 128)
    params = pltpu.CompilerParams(vmem_limit_bytes=24 * 2**20)
    table = jax.ShapeDtypeStruct(slots.shape, jnp.int32)
    staged = (pltpu.SMEM(slots.shape, jnp.int32), pltpu.SemaphoreType.DMA)
    x_first, x_last, y_first, y_last = pl.pallas_call(
        functools.partial(faces_kernel, (size_x, size_y)),
        out_shape=(face_x, face_x, face_y, face_y),
        in_specs=[anywhere],
        out_specs=(inside,) * 4,
        scratch_shapes=[
            VMEM((size_z // 128, cells, 128), F32),
            pltpu.SemaphoreType.DMA((size_z // 128,)),
        ],
        compiler_params=pltpu.CompilerParams(vmem_limit_bytes=24 * 2**20),
        name="faces",
    )(vel)
    chunk, slots, own = pl.pallas_call(
        functools.partial(pack_kernel, (count_d, width)),
        out_shape=(jax.ShapeDtypeStruct((count_d, width + 16, 128), BF16), table, table),
        in_specs=[anywhere, inside, inside, inside],
        out_specs=(inside,) * 3,
        scratch_shapes=[VMEM((count_d * 16, 128), F32), pltpu.SemaphoreType.DMA],
        compiler_params=params,
        name="pack",
    )(block_w, wanted, slots, own)

    def ring(x, axis, step):
        size = lax.axis_size(axis)
        return lax.ppermute(x, axis, [(i, (i + step) % size) for i in range(size)])

    def swap(x, mask):
        return lax.ppermute(x, "gx", [(i, i ^ mask) for i in range(lax.axis_size("gx"))])

    x_before = ring(x_last, "gx", 1)
    x_after = ring(x_first, "gx", -1)
    y_before = ring(y_last, "gy", 1)
    y_after = ring(y_first, "gy", -1)
    arrived = lax.all_to_all(chunk, "gx", split_axis=0, concat_axis=0, tiled=True)
    field, keep, give = pl.pallas_call(
        functools.partial(predict_kernel, dims),
        out_shape=(jax.ShapeDtypeStruct(padded, F32), half, half),
        in_specs=[inside] * 7,
        out_specs=(inside,) * 3,
        scratch_shapes=[VMEM((group * high * 8, 128), F32), *staged],
        compiler_params=params,
        name="predict",
    )(slots, vel, x_before, x_after, y_before, y_after, jnp.asarray(shifts()))
    first = swap(give, 1)
    received = [swap(jnp.stack([keep[k], first[k]]), 2 * k) for k in range(1, count_d // 2)]
    out, token = pl.pallas_call(
        functools.partial(spread_kernel, dims),
        out_shape=(jax.ShapeDtypeStruct((cells, size_z), F32), jax.ShapeDtypeStruct((8, 128), F32)),
        in_specs=[inside] * 6,
        out_specs=(anywhere, inside),
        scratch_shapes=[
            VMEM(padded, F32),
            VMEM((group * high * 8, 128), F32),
            VMEM((group * high, 128), F32),
            staged[0],
            pltpu.SemaphoreType.DMA((2 + size_z // 128,)),
        ],
        compiler_params=params,
        cost_estimate=pl.CostEstimate(flops=10**8, bytes_accessed=4 * 10**6, transcendentals=0),
        name="spread",
    )(slots, field, keep, give, arrived, jnp.asarray(shifts().T))
    force = pl.pallas_call(
        functools.partial(owner_kernel, dims),
        out_shape=jax.ShapeDtypeStruct((3, count_d, width), F32),
        in_specs=[inside] * (5 + count_d // 2),
        out_specs=inside,
        scratch_shapes=[VMEM((count_d, high, 128), BF16), *staged],
        compiler_params=params,
        name="owner",
    )(own, token, wanted, block_w, keep, first, *received)
    return out.reshape(velocity.shape), jnp.transpose(force, (1, 0, 2))[None, None]


def solution(mesh):
    return jax.shard_map(
        shards,
        mesh=mesh,
        in_specs=(
            P(None, "gx", "gy", None),
            P("gx", "gy", None, None, None, None),
            P("gx", "gy", None, None, None),
            P("gx", "gy", None, None),
            P("gx", "gy", None, None),
        ),
        out_specs=(P(None, "gx", "gy", None), P("gx", "gy", None, None, None)),
        check_vma=False,
    )
```

```python
import functools

import jax
import jax.numpy as jnp
import ml_dtypes
import numpy as np
from jax import lax
from jax.experimental import pallas as pl
from jax.experimental.pallas import tpu as pltpu
from jax.sharding import PartitionSpec as P

time_step = 0.05
viscosity = 0.5
spread_gain = 0.5

VMEM = pltpu.VMEM
F32 = jnp.float32
BF16 = jnp.bfloat16


def each(count, body, flat=False):
    if flat or count == 1:
        for i in range(count):
            body(i)
    else:

        def step(i, carry):
            body(i)
            return carry

        lax.fori_loop(0, count, step, 0)


def faces_kernel(dims, vel, y_first, y_last, held, sems):
    size_x, size_y = dims
    halves = held.shape[0]
    moves = [
        pltpu.make_async_copy(vel.at[:, pl.ds(part * 128, 128)], held.at[part], sems.at[part])
        for part in range(halves)
    ]
    for move in moves:
        move.start()
    plane = size_x * size_y
    for part in range(halves):
        moves[part].wait()
        lanes = pl.ds(part * 128, 128)
        for c in range(3):
            y_first[c, :, lanes] = held[part, pl.ds(c * plane, size_x, stride=size_y), :]
            y_last[c, :, lanes] = held[part, pl.ds(c * plane + size_y - 1, size_x, stride=size_y), :]


def pack_kernel(dims, w, t, slots, own, chunk, slots_out, own_out, rows, packed, sems):
    slots_out[...] = slots[...]
    own_out[...] = own[...]
    count_d, width = dims
    move_w = pltpu.make_async_copy(w, chunk.at[:, pl.ds(0, width), :], sems.at[0])
    move_w.start()
    rows[...] = jnp.zeros_like(rows)
    rest = jnp.zeros((count_d, 256 - width), F32)
    for c in range(3):
        values = t[c].astype(F32)
        rows[pl.ds(c, count_d, stride=16), :] = values[:, 0:128]
        rows[pl.ds(8 + c, count_d, stride=16), :] = jnp.concatenate([values[:, 128:width], rest], axis=1)
    packed[...] = rows[...].astype(BF16).reshape(count_d, 16, 128)
    move_t = pltpu.make_async_copy(packed, chunk.at[:, pl.ds(width, 16), :], sems.at[1])
    move_t.start()
    move_t.wait()
    move_w.wait()


def split(x, size):
    if size & (size - 1) == 0:
        return lax.shift_right_logical(x, size.bit_length() - 1), x & (size - 1)
    return lax.div(x, size), lax.rem(x, size)


def shifts():
    piece = np.arange(1024)[:, None]
    m = piece % 128
    hit = (m % 64 < 8) & (np.arange(128)[None, :] == m + 8 * (piece // 128))
    return hit.astype(ml_dtypes.bfloat16)


def locate(dims, slots, i, s):
    size_x, size_y, size_z = dims[:3]
    safe = jnp.maximum(slots[0, s, 0, i], 0)
    rest, qz = split(safe, size_z // 8)
    qx, qy = split(rest, size_y // 4)
    half, layer = split(qz, 16)
    first = 8 + qx * (4 * size_y) + qy * 4
    return half, first, 8 * layer


def windows(dims, half, first, c):
    size_x, size_y = dims[:2]
    return [(half, pl.ds(first + ((c * size_x + ax) * size_y - 4 * (ax % 2)), 8)) for ax in range(4)]


def low_halves():
    lane = lax.broadcasted_iota(jnp.int32, (8, 128), 1)
    sub = lax.broadcasted_iota(jnp.int32, (8, 128), 0)
    return lane < 64, sub < 4


def select_slots(product, slot_of, count_s):
    interp = None
    for s in range(count_s):
        part = product[s // 2 * 8 : s // 2 * 8 + 8]
        if s % 2:
            part = pltpu.roll(part, 4, 0)
        interp = part if s == 0 else jnp.where(slot_of == s, part, interp)
    return interp


def predict_kernel(
    dims, table, vel, x_before, x_after, y_before, y_after, gathers, field, keep, give, stage, slots, sem,
):
    size_x, size_y, size_z, count_d, count_s, width = dims
    halves = size_z // 128
    me = lax.axis_index("gx")
    move = pltpu.make_async_copy(table, slots, sem)
    move.start()

    row = lax.broadcasted_iota(jnp.int32, (size_y, size_z), 0)
    col = lax.broadcasted_iota(jnp.int32, (size_y, size_z), 1)

    def stencil(x):
        center = [vel[pl.ds((c * size_x + x) * size_y, size_y), :] for c in range(3)]
        for c in range(3):
            base = (c * size_x + x) * size_y
            here = center[c]
            fore = x_after[c] if x == size_x - 1 else vel[pl.ds(base + size_y, size_y), :]
            back = x_before[c] if x == 0 else vel[pl.ds(base - size_y, size_y), :]
            total = (fore + back) - center[0] * (fore - back)
            right = jnp.where(row == size_y - 1, y_after[c, pl.ds(x, 1), :], pltpu.roll(here, size_y - 1, 0))
            left = jnp.where(row == 0, y_before[c, pl.ds(x, 1), :], pltpu.roll(here, 1, 0))
            total = total + ((right + left) - center[1] * (right - left))
            top = jnp.where(col == size_z - 1, 0.0, pltpu.roll(here, size_z - 1, 1))
            bottom = jnp.where(col == 0, 0.0, pltpu.roll(here, 1, 1))
            total = total + ((top + bottom) - center[2] * (top - bottom))
            base = 8 + (c * size_x + x) * size_y
            result = (1.0 - 6.0 * time_step * viscosity) * center[c] + (0.5 * time_step) * total
            for part in range(halves):
                field[part, pl.ds(base, size_y), :] = result[:, part * 128 : part * 128 + 128]

    each(size_x, stencil, True)

    move.wait()
    low_lane, low_sub = low_halves()
    group = 8 if count_d % 8 == 0 else count_d
    high = keep.shape[1]
    lines = group * high

    def gather(i, g):
        for s in range(count_s):
            half, first, shift = locate(dims, slots, i, s)
            for c in range(3):
                w = [field[k, at, :] for k, at in windows(dims, half, first, c)]
                near = pltpu.roll(jnp.where(low_sub, w[0], w[1]), (128 - shift) & 127, 1)
                far = pltpu.roll(jnp.where(low_sub, w[2], w[3]), (192 - shift) & 127, 1)
                stage[pl.ds((g * high + s * 4 + c) * 8, 8), :] = jnp.where(low_lane, near, far)

    def batch(k):
        for g in range(group):
            gather(me ^ (k * group + g), g)
        picked = jnp.concatenate([stage[pl.ds(r, lines, stride=8), :] for r in range(8)], axis=1)
        picked = jnp.dot(picked.astype(BF16), gathers[...], preferred_element_type=F32).astype(BF16)
        for g in range(group):
            (give if g % 2 else keep)[k * (group // 2) + g // 2] = picked[g * high : (g + 1) * high]

    stage[...] = jnp.zeros_like(stage)
    each(count_d // group, batch)


def spread_kernel(
    dims, table, own_table, before, keep, give, blocks, scatters, out, live_out, field, stage, chosen,
    slots, own, sems,
):
    size_x, size_y, size_z, count_d, count_s, width = dims
    cells = 3 * size_x * size_y
    halves = size_z // 128
    me = lax.axis_index("gx")
    move_field = pltpu.make_async_copy(before, field, sems.at[0])
    move_slots = pltpu.make_async_copy(table, slots, sems.at[1])
    move_own = pltpu.make_async_copy(own_table, own, sems.at[2])
    move_slots.start()
    move_own.start()
    move_field.start()
    low_lane, low_sub = low_halves()
    group = 8 if count_d % 8 == 0 else count_d
    high = keep.shape[1]
    lines = group * high
    slot_of = lax.broadcasted_iota(jnp.int32, (8, width), 1) // (width // count_s)
    low_row = lax.broadcasted_iota(jnp.int32, (8, width), 0) < 4

    def interpolate(i, block):
        return lax.dot_general(
            block, blocks[i, 0:width, :], (((1,), (1,)), ((), ())), preferred_element_type=F32
        )

    def force(i, product):
        tail = blocks[i, width : width + 16, :].astype(F32)
        target = jnp.concatenate([tail[0:8, :], tail[8:16, 0 : width - 128]], axis=1)
        interp = select_slots(product, slot_of, count_s)
        live = jnp.full((8, width), slots[0, 0, 0, i], jnp.int32)
        for s in range(1, count_s):
            live = jnp.where(slot_of == s, slots[0, s, 0, i], live)
        value = jnp.where(live >= 0, (target - interp) / time_step, 0.0)
        swapped = pltpu.roll(value, 4, 0)
        rows = []
        for first in range(0, high // 4, 2):
            lower = jnp.where(slot_of == first, value, 0.0)
            upper = jnp.where(slot_of == first + 1, swapped, 0.0)
            rows.append(jnp.where(low_row, lower, upper))
        return jnp.concatenate(rows, axis=0).astype(BF16)

    def scatter(i, g):
        for s in range(count_s):
            half, first, shift = locate(dims, slots, i, s)
            for c in range(3):
                both = stage[pl.ds((g * high + s * 4 + c) * 8, 8), :]
                near = pltpu.roll(jnp.where(low_lane, both, 0.0), shift, 1)
                far = pltpu.roll(jnp.where(low_lane, 0.0, both), (shift + 64) & 127, 1)
                spots = windows(dims, half, first, c)
                pieces = [
                    jnp.where(low_sub, near, 0.0), jnp.where(low_sub, 0.0, near),
                    jnp.where(low_sub, far, 0.0), jnp.where(low_sub, 0.0, far),
                ]
                sums = [field[k, at, :] + piece for (k, at), piece in zip(spots, pieces)]
                for (k, at), total in zip(spots, sums):
                    field[k, at, :] = total

    row = lax.broadcasted_iota(jnp.int32, (group, width), 0)
    column_slot = lax.broadcasted_iota(jnp.int32, (group, width), 1) // (width // count_s)

    def mark_live(k):
        live = jnp.full((group, width), -1, jnp.int32)
        for g in range(group):
            for s in range(count_s):
                live = jnp.where((row == g) & (column_slot == s), own[0, s, 0, k * group + g], live)
        live_out[pl.ds(k * group, group), :] = live

    def batch(k):
        owners = [me ^ (k * group + g) for g in range(group)]
        products = [
            interpolate(owners[g], (give if g % 2 else keep)[k * (group // 2) + g // 2])
            for g in range(group)
        ]
        if count_d == group:
            move_slots.wait()
            move_own.wait()
        forces = [force(owners[g], products[g]) for g in range(group)]
        for g in range(group):
            chosen[pl.ds(g * high, high), :] = jnp.dot(
                forces[g], blocks[owners[g], 0:width, :], preferred_element_type=F32
            )
        mark_live(k)
        rows = chosen[...] * (time_step * spread_gain)
        upper = rows.astype(BF16)
        lower = (rows - upper.astype(F32)).astype(BF16)
        pieces = jnp.dot(upper, scatters[...], preferred_element_type=F32)
        pieces = pieces + jnp.dot(lower, scatters[...], preferred_element_type=F32)
        for r in range(8):
            stage[pl.ds(r, lines, stride=8), :] = pieces[:, r * 128 : r * 128 + 128]
        if count_d == group:
            move_field.wait()
        for g in range(group):
            scatter(owners[g], g)

    if count_d != group:
        move_slots.wait()
        move_own.wait()
        move_field.wait()
    each(count_d // group, batch)
    moves = [
        pltpu.make_async_copy(
            field.at[part, pl.ds(8, cells), :], out.at[:, pl.ds(part * 128, 128)], sems.at[3 + part]
        )
        for part in range(halves)
    ]
    for move in moves:
        move.start()
    for move in moves:
        move.wait()


def owner_kernel(dims, live, targets, block_w, keep, first, *rest):
    size_x, size_y, size_z, count_d, count_s, width = dims
    received, (out, picked) = rest[:-2], rest[-2:]
    me = lax.axis_index("gx")
    group = 8 if count_d % 8 == 0 else count_d
    slot_of = lax.broadcasted_iota(jnp.int32, (8, width), 1) // (width // count_s)
    row = lax.broadcasted_iota(jnp.int32, (group, width), 0)
    picked[0] = keep[0]
    picked[1] = first[0]
    for k, pair in enumerate(received):
        picked[2 * k + 2] = pair[0]
        picked[2 * k + 3] = pair[1]

    def batch(k):
        products = [
            lax.dot_general(
                picked[me ^ (k * group + g)], block_w[k * group + g],
                (((1,), (1,)), ((), ())), preferred_element_type=F32,
            )
            for g in range(group)
        ]
        interp = [jnp.zeros((group, width), F32) for c in range(3)]
        for g in range(group):
            lines = select_slots(products[g], slot_of, count_s)
            for c in range(3):
                interp[c] = jnp.where(row == g, lines[c : c + 1], interp[c])
        for c in range(3):
            at = pl.ds(k * group, group)
            target = targets[c, at, :].astype(F32)
            out[c, at, :] = jnp.where(live[at, :] >= 0, (target - interp[c]) / time_step, 0.0)

    each(count_d // group, batch)


def shards(velocity, weights, targets, owner_list, slot_patch):
    size_x, size_y, size_z = velocity.shape[1:]
    count_d, count_s, markers = weights.shape[2:5]
    width = count_s * markers
    cells = 3 * size_x * size_y
    vel = velocity.reshape(cells, size_z)
    block_w = weights.reshape(count_d, width, 128)
    wanted = jnp.transpose(targets[0, 0], (1, 0, 2))
    slots = jnp.transpose(slot_patch, (0, 3, 1, 2))
    own = jnp.transpose(owner_list, (0, 3, 1, 2))
    dims = (size_x, size_y, size_z, count_d, count_s, width)
    group = 8 if count_d % 8 == 0 else count_d
    high = -(-count_s * 4 // 16) * 16
    anywhere = pl.BlockSpec(memory_space=pl.ANY)
    inside = pl.BlockSpec(memory_space=VMEM)
    face_y = jax.ShapeDtypeStruct((3, size_x, size_z), F32)
    half = jax.ShapeDtypeStruct((count_d // 2, high, 128), BF16)
    padded = (size_z // 128, cells + 16, 128)
    params = pltpu.CompilerParams(vmem_limit_bytes=24 * 2**20)
    table = jax.ShapeDtypeStruct(slots.shape, jnp.int32)
    staged = (pltpu.SMEM(slots.shape, jnp.int32), pltpu.SemaphoreType.DMA)
    x_first, x_last = velocity[:, 0], velocity[:, size_x - 1]
    y_first, y_last = pl.pallas_call(
        functools.partial(faces_kernel, (size_x, size_y)),
        out_shape=(face_y, face_y),
        in_specs=[anywhere],
        out_specs=(inside,) * 2,
        scratch_shapes=[
            VMEM((size_z // 128, cells, 128), F32),
            pltpu.SemaphoreType.DMA((size_z // 128,)),
        ],
        compiler_params=pltpu.CompilerParams(vmem_limit_bytes=24 * 2**20),
        name="faces",
    )(vel)
    chunk, slots, own = pl.pallas_call(
        functools.partial(pack_kernel, (count_d, width)),
        out_shape=(jax.ShapeDtypeStruct((count_d, width + 16, 128), BF16), table, table),
        in_specs=[inside, inside, inside, inside],
        out_specs=(anywhere, inside, inside),
        scratch_shapes=[
            VMEM((count_d * 16, 128), F32),
            VMEM((count_d, 16, 128), BF16),
            pltpu.SemaphoreType.DMA((2,)),
        ],
        compiler_params=params,
        name="pack",
    )(block_w, wanted, slots, own)

    def ring(x, axis, step):
        size = lax.axis_size(axis)
        return lax.ppermute(x, axis, [(i, (i + step) % size) for i in range(size)])

    def swap(x, mask):
        return lax.ppermute(x, "gx", [(i, i ^ mask) for i in range(lax.axis_size("gx"))])

    x_before = ring(x_last, "gx", 1)
    x_after = ring(x_first, "gx", -1)
    y_before = ring(y_last, "gy", 1)
    y_after = ring(y_first, "gy", -1)
    arrived = lax.all_to_all(chunk, "gx", split_axis=0, concat_axis=0, tiled=True)
    field, keep, give = pl.pallas_call(
        functools.partial(predict_kernel, dims),
        out_shape=(jax.ShapeDtypeStruct(padded, F32), half, half),
        in_specs=[inside] * 7,
        out_specs=(inside,) * 3,
        scratch_shapes=[VMEM((group * high * 8, 128), F32), *staged],
        compiler_params=params,
        name="predict",
    )(slots, vel, x_before, x_after, y_before, y_after, jnp.asarray(shifts()))
    first = swap(give, 1)
    received = [swap(jnp.stack([keep[k], first[k]]), 2 * k) for k in range(1, count_d // 2)]
    out, live = pl.pallas_call(
        functools.partial(spread_kernel, dims),
        out_shape=(jax.ShapeDtypeStruct((cells, size_z), F32), jax.ShapeDtypeStruct((count_d, width), jnp.int32)),
        in_specs=[inside] * 7,
        out_specs=(anywhere, inside),
        scratch_shapes=[
            VMEM(padded, F32),
            VMEM((group * high * 8, 128), F32),
            VMEM((group * high, 128), F32),
            staged[0],
            staged[0],
            pltpu.SemaphoreType.DMA((3 + size_z // 128,)),
        ],
        compiler_params=params,
        cost_estimate=pl.CostEstimate(flops=10**8, bytes_accessed=4 * 10**6, transcendentals=0),
        name="spread",
    )(slots, own, field, keep, give, arrived, jnp.asarray(shifts().T))
    force = pl.pallas_call(
        functools.partial(owner_kernel, dims),
        out_shape=jax.ShapeDtypeStruct((3, count_d, width), F32),
        in_specs=[inside] * (4 + count_d // 2),
        out_specs=inside,
        scratch_shapes=[VMEM((count_d, high, 128), BF16)],
        compiler_params=params,
        name="owner",
    )(live, wanted, block_w, keep, first, *received)
    return out.reshape(velocity.shape), jnp.transpose(force, (1, 0, 2))[None, None]


def solution(mesh):
    return jax.shard_map(
        shards,
        mesh=mesh,
        in_specs=(
            P(None, "gx", "gy", None),
            P("gx", "gy", None, None, None, None),
            P("gx", "gy", None, None, None),
            P("gx", "gy", None, None),
            P("gx", "gy", None, None),
        ),
        out_specs=(P(None, "gx", "gy", None), P("gx", "gy", None, None, None)),
        check_vma=False,
    )
```

```python
import functools

import jax
import jax.numpy as jnp
import ml_dtypes
import numpy as np
from jax import lax
from jax.experimental import pallas as pl
from jax.experimental.pallas import tpu as pltpu
from jax.sharding import PartitionSpec as P

time_step = 0.05
viscosity = 0.5
spread_gain = 0.5

VMEM = pltpu.VMEM
F32 = jnp.float32
BF16 = jnp.bfloat16


def each(count, body, flat=False):
    if flat or count == 1:
        for i in range(count):
            body(i)
    else:

        def step(i, carry):
            body(i)
            return carry

        lax.fori_loop(0, count, step, 0)


def faces_kernel(dims, vel, y_first, y_last, held, sems):
    size_x, size_y = dims
    halves = held.shape[0]
    moves = [
        pltpu.make_async_copy(vel.at[:, pl.ds(part * 128, 128)], held.at[part], sems.at[part])
        for part in range(halves)
    ]
    for move in moves:
        move.start()
    plane = size_x * size_y
    for part in range(halves):
        moves[part].wait()
        lanes = pl.ds(part * 128, 128)
        for c in range(3):
            y_first[c, :, lanes] = held[part, pl.ds(c * plane, size_x, stride=size_y), :]
            y_last[c, :, lanes] = held[part, pl.ds(c * plane + size_y - 1, size_x, stride=size_y), :]


def pack_kernel(dims, w, t, slots, own, chunk, slots_out, own_out, rows, packed, sems):
    slots_out[...] = slots[...]
    own_out[...] = own[...]
    count_d, width = dims
    move_w = pltpu.make_async_copy(w, chunk.at[:, pl.ds(0, width), :], sems.at[0])
    move_w.start()
    rows[...] = jnp.zeros_like(rows)
    rest = jnp.zeros((count_d, 256 - width), F32)
    for c in range(3):
        values = t[c].astype(F32)
        rows[pl.ds(c, count_d, stride=16), :] = values[:, 0:128]
        rows[pl.ds(8 + c, count_d, stride=16), :] = jnp.concatenate([values[:, 128:width], rest], axis=1)
    packed[...] = rows[...].astype(BF16).reshape(count_d, 16, 128)
    move_t = pltpu.make_async_copy(packed, chunk.at[:, pl.ds(width, 16), :], sems.at[1])
    move_t.start()
    move_t.wait()
    move_w.wait()


def split(x, size):
    if size & (size - 1) == 0:
        return lax.shift_right_logical(x, size.bit_length() - 1), x & (size - 1)
    return lax.div(x, size), lax.rem(x, size)


def shifts():
    piece = np.arange(1024)[:, None]
    m = piece % 128
    hit = (m % 64 < 8) & (np.arange(128)[None, :] == m + 8 * (piece // 128))
    return hit.astype(ml_dtypes.bfloat16)


def locate(dims, slots, i, s):
    size_x, size_y, size_z = dims[:3]
    safe = jnp.maximum(slots[0, s, 0, i], 0)
    rest, qz = split(safe, size_z // 8)
    qx, qy = split(rest, size_y // 4)
    half, layer = split(qz, 16)
    first = 8 + qx * (4 * size_y) + qy * 4
    return half, first, 8 * layer


def windows(dims, half, first, c):
    size_x, size_y = dims[:2]
    return [(half, pl.ds(first + ((c * size_x + ax) * size_y - 4 * (ax % 2)), 8)) for ax in range(4)]


def low_halves():
    lane = lax.broadcasted_iota(jnp.int32, (8, 128), 1)
    sub = lax.broadcasted_iota(jnp.int32, (8, 128), 0)
    return lane < 64, sub < 4


def select_slots(product, slot_of, count_s):
    interp = None
    for s in range(count_s):
        part = product[s // 2 * 8 : s // 2 * 8 + 8]
        if s % 2:
            part = pltpu.roll(part, 4, 0)
        interp = part if s == 0 else jnp.where(slot_of == s, part, interp)
    return interp


def predict_kernel(
    dims, table, vel, x_before, x_after, y_before, y_after, gathers, field, keep, give, stage, slots, sem,
):
    size_x, size_y, size_z, count_d, count_s, width = dims
    halves = size_z // 128
    me = lax.axis_index("gx")
    move = pltpu.make_async_copy(table, slots, sem)
    move.start()

    row = lax.broadcasted_iota(jnp.int32, (size_y, size_z), 0)
    col = lax.broadcasted_iota(jnp.int32, (size_y, size_z), 1)

    def stencil(x):
        center = [vel[pl.ds((c * size_x + x) * size_y, size_y), :] for c in range(3)]
        for c in range(3):
            base = (c * size_x + x) * size_y
            here = center[c]
            fore = x_after[c] if x == size_x - 1 else vel[pl.ds(base + size_y, size_y), :]
            back = x_before[c] if x == 0 else vel[pl.ds(base - size_y, size_y), :]
            total = (fore + back) - center[0] * (fore - back)
            right = jnp.where(row == size_y - 1, y_after[c, pl.ds(x, 1), :], pltpu.roll(here, size_y - 1, 0))
            left = jnp.where(row == 0, y_before[c, pl.ds(x, 1), :], pltpu.roll(here, 1, 0))
            total = total + ((right + left) - center[1] * (right - left))
            top = jnp.where(col == size_z - 1, 0.0, pltpu.roll(here, size_z - 1, 1))
            bottom = jnp.where(col == 0, 0.0, pltpu.roll(here, 1, 1))
            total = total + ((top + bottom) - center[2] * (top - bottom))
            base = 8 + (c * size_x + x) * size_y
            result = (1.0 - 6.0 * time_step * viscosity) * center[c] + (0.5 * time_step) * total
            for part in range(halves):
                field[part, pl.ds(base, size_y), :] = result[:, part * 128 : part * 128 + 128]

    each(size_x, stencil, True)

    move.wait()
    low_lane, low_sub = low_halves()
    group = 8 if count_d % 8 == 0 else count_d
    high = keep.shape[1]
    lines = group * high

    def gather(i, g):
        for s in range(count_s):
            half, first, shift = locate(dims, slots, i, s)
            for c in range(3):
                w = [field[k, at, :] for k, at in windows(dims, half, first, c)]
                near = pltpu.roll(jnp.where(low_sub, w[0], w[1]), (128 - shift) & 127, 1)
                far = pltpu.roll(jnp.where(low_sub, w[2], w[3]), (192 - shift) & 127, 1)
                stage[pl.ds((g * high + s * 4 + c) * 8, 8), :] = jnp.where(low_lane, near, far)

    def batch(k):
        for g in range(group):
            gather(me ^ (k * group + g), g)
        picked = jnp.concatenate([stage[pl.ds(r, lines, stride=8), :] for r in range(8)], axis=1)
        picked = jnp.dot(picked.astype(BF16), gathers[...], preferred_element_type=F32).astype(BF16)
        for g in range(group):
            (give if g % 2 else keep)[k * (group // 2) + g // 2] = picked[g * high : (g + 1) * high]

    stage[...] = jnp.zeros_like(stage)
    each(count_d // group, batch)


def spread_kernel(
    dims, table, own_table, before, keep, give, blocks, scatters, out, live_out, field, stage, chosen,
    slots, own, sems,
):
    size_x, size_y, size_z, count_d, count_s, width = dims
    cells = 3 * size_x * size_y
    halves = size_z // 128
    me = lax.axis_index("gx")
    move_field = pltpu.make_async_copy(before, field, sems.at[0])
    move_slots = pltpu.make_async_copy(table, slots, sems.at[1])
    move_own = pltpu.make_async_copy(own_table, own, sems.at[2])
    move_slots.start()
    move_own.start()
    move_field.start()
    low_lane, low_sub = low_halves()
    group = 8 if count_d % 8 == 0 else count_d
    high = keep.shape[1]
    lines = group * high
    slot_of = lax.broadcasted_iota(jnp.int32, (8, width), 1) // (width // count_s)
    low_row = lax.broadcasted_iota(jnp.int32, (8, width), 0) < 4

    def interpolate(i, block):
        return lax.dot_general(
            block, blocks[i, 0:width, :], (((1,), (1,)), ((), ())), preferred_element_type=F32
        )

    def force(i, product):
        tail = blocks[i, width : width + 16, :].astype(F32)
        target = jnp.concatenate([tail[0:8, :], tail[8:16, 0 : width - 128]], axis=1)
        interp = select_slots(product, slot_of, count_s)
        live = jnp.full((8, width), slots[0, 0, 0, i], jnp.int32)
        for s in range(1, count_s):
            live = jnp.where(slot_of == s, slots[0, s, 0, i], live)
        value = jnp.where(live >= 0, (target - interp) / time_step, 0.0)
        swapped = pltpu.roll(value, 4, 0)
        rows = []
        for first in range(0, high // 4, 2):
            lower = jnp.where(slot_of == first, value, 0.0)
            upper = jnp.where(slot_of == first + 1, swapped, 0.0)
            rows.append(jnp.where(low_row, lower, upper))
        return jnp.concatenate(rows, axis=0).astype(BF16)

    def scatter(i, g):
        for s in range(count_s):
            half, first, shift = locate(dims, slots, i, s)
            for c in range(3):
                both = stage[pl.ds((g * high + s * 4 + c) * 8, 8), :]
                near = pltpu.roll(jnp.where(low_lane, both, 0.0), shift, 1)
                far = pltpu.roll(jnp.where(low_lane, 0.0, both), (shift + 64) & 127, 1)
                spots = windows(dims, half, first, c)
                pieces = [
                    jnp.where(low_sub, near, 0.0), jnp.where(low_sub, 0.0, near),
                    jnp.where(low_sub, far, 0.0), jnp.where(low_sub, 0.0, far),
                ]
                sums = [field[k, at, :] + piece for (k, at), piece in zip(spots, pieces)]
                for (k, at), total in zip(spots, sums):
                    field[k, at, :] = total

    row = lax.broadcasted_iota(jnp.int32, (group, width), 0)
    column_slot = lax.broadcasted_iota(jnp.int32, (group, width), 1) // (width // count_s)

    def mark_live(k):
        live = jnp.full((group, width), -1, jnp.int32)
        for g in range(group):
            for s in range(count_s):
                live = jnp.where((row == g) & (column_slot == s), own[0, s, 0, k * group + g], live)
        live_out[pl.ds(k * group, group), :] = live

    def batch(k):
        owners = [me ^ (k * group + g) for g in range(group)]
        products = [
            interpolate(owners[g], (give if g % 2 else keep)[k * (group // 2) + g // 2])
            for g in range(group)
        ]
        if count_d == group:
            move_slots.wait()
            move_own.wait()
        forces = [force(owners[g], products[g]) for g in range(group)]
        for g in range(group):
            chosen[pl.ds(g * high, high), :] = jnp.dot(
                forces[g], blocks[owners[g], 0:width, :], preferred_element_type=F32
            )
        mark_live(k)
        rows = chosen[...] * (time_step * spread_gain)
        upper = rows.astype(BF16)
        lower = (rows - upper.astype(F32)).astype(BF16)
        both = jnp.concatenate([upper, lower], axis=1)
        pieces = jnp.dot(both, scatters[...], preferred_element_type=F32)
        for r in range(8):
            stage[pl.ds(r, lines, stride=8), :] = pieces[:, r * 128 : r * 128 + 128]
        if count_d == group:
            move_field.wait()
        for g in range(group):
            scatter(owners[g], g)

    if count_d != group:
        move_slots.wait()
        move_own.wait()
        move_field.wait()
    each(count_d // group, batch)
    moves = [
        pltpu.make_async_copy(
            field.at[part, pl.ds(8, cells), :], out.at[:, pl.ds(part * 128, 128)], sems.at[3 + part]
        )
        for part in range(halves)
    ]
    for move in moves:
        move.start()
    for move in moves:
        move.wait()


def owner_kernel(dims, live, targets, block_w, keep, first, *rest):
    size_x, size_y, size_z, count_d, count_s, width = dims
    received, (out, picked) = rest[:-2], rest[-2:]
    me = lax.axis_index("gx")
    group = 8 if count_d % 8 == 0 else count_d
    slot_of = lax.broadcasted_iota(jnp.int32, (8, width), 1) // (width // count_s)
    row = lax.broadcasted_iota(jnp.int32, (group, width), 0)
    picked[0] = keep[0]
    picked[1] = first[0]
    for k, pair in enumerate(received):
        picked[2 * k + 2] = pair[0]
        picked[2 * k + 3] = pair[1]

    def batch(k):
        products = [
            lax.dot_general(
                picked[me ^ (k * group + g)], block_w[k * group + g],
                (((1,), (1,)), ((), ())), preferred_element_type=F32,
            )
            for g in range(group)
        ]
        interp = [jnp.zeros((group, width), F32) for c in range(3)]
        for g in range(group):
            lines = select_slots(products[g], slot_of, count_s)
            for c in range(3):
                interp[c] = jnp.where(row == g, lines[c : c + 1], interp[c])
        for c in range(3):
            at = pl.ds(k * group, group)
            target = (targets[c] if count_d == group else targets[c, at, :]).astype(F32)
            out[c, at, :] = jnp.where(live[at, :] >= 0, (target - interp[c]) / time_step, 0.0)

    each(count_d // group, batch)


def shards(velocity, weights, targets, owner_list, slot_patch):
    size_x, size_y, size_z = velocity.shape[1:]
    count_d, count_s, markers = weights.shape[2:5]
    width = count_s * markers
    cells = 3 * size_x * size_y
    vel = velocity.reshape(cells, size_z)
    block_w = weights.reshape(count_d, width, 128)
    wanted = jnp.transpose(targets[0, 0], (1, 0, 2))
    slots = jnp.transpose(slot_patch, (0, 3, 1, 2))
    own = jnp.transpose(owner_list, (0, 3, 1, 2))
    dims = (size_x, size_y, size_z, count_d, count_s, width)
    group = 8 if count_d % 8 == 0 else count_d
    high = -(-count_s * 4 // 16) * 16
    anywhere = pl.BlockSpec(memory_space=pl.ANY)
    inside = pl.BlockSpec(memory_space=VMEM)
    face_y = jax.ShapeDtypeStruct((3, size_x, size_z), F32)
    half = jax.ShapeDtypeStruct((count_d // 2, high, 128), BF16)
    padded = (size_z // 128, cells + 16, 128)
    params = pltpu.CompilerParams(vmem_limit_bytes=24 * 2**20)
    table = jax.ShapeDtypeStruct(slots.shape, jnp.int32)
    staged = (pltpu.SMEM(slots.shape, jnp.int32), pltpu.SemaphoreType.DMA)
    x_first, x_last = velocity[:, 0], velocity[:, size_x - 1]
    y_first, y_last = pl.pallas_call(
        functools.partial(faces_kernel, (size_x, size_y)),
        out_shape=(face_y, face_y),
        in_specs=[anywhere],
        out_specs=(inside,) * 2,
        scratch_shapes=[
            VMEM((size_z // 128, cells, 128), F32),
            pltpu.SemaphoreType.DMA((size_z // 128,)),
        ],
        compiler_params=pltpu.CompilerParams(vmem_limit_bytes=24 * 2**20),
        name="faces",
    )(vel)
    chunk, slots, own = pl.pallas_call(
        functools.partial(pack_kernel, (count_d, width)),
        out_shape=(jax.ShapeDtypeStruct((count_d, width + 16, 128), BF16), table, table),
        in_specs=[inside, inside, inside, inside],
        out_specs=(anywhere, inside, inside),
        scratch_shapes=[
            VMEM((count_d * 16, 128), F32),
            VMEM((count_d, 16, 128), BF16),
            pltpu.SemaphoreType.DMA((2,)),
        ],
        compiler_params=params,
        name="pack",
    )(block_w, wanted, slots, own)

    def ring(x, axis, step):
        size = lax.axis_size(axis)
        return lax.ppermute(x, axis, [(i, (i + step) % size) for i in range(size)])

    def swap(x, mask):
        return lax.ppermute(x, "gx", [(i, i ^ mask) for i in range(lax.axis_size("gx"))])

    x_before = ring(x_last, "gx", 1)
    x_after = ring(x_first, "gx", -1)
    y_before = ring(y_last, "gy", 1)
    y_after = ring(y_first, "gy", -1)
    arrived = lax.all_to_all(chunk, "gx", split_axis=0, concat_axis=0, tiled=True)
    field, keep, give = pl.pallas_call(
        functools.partial(predict_kernel, dims),
        out_shape=(jax.ShapeDtypeStruct(padded, F32), half, half),
        in_specs=[inside] * 7,
        out_specs=(inside,) * 3,
        scratch_shapes=[VMEM((group * high * 8, 128), F32), *staged],
        compiler_params=params,
        name="predict",
    )(slots, vel, x_before, x_after, y_before, y_after, jnp.asarray(shifts()))
    first = swap(give, 1)
    received = [swap(jnp.stack([keep[k], first[k]]), 2 * k) for k in range(1, count_d // 2)]
    out, live = pl.pallas_call(
        functools.partial(spread_kernel, dims),
        out_shape=(jax.ShapeDtypeStruct((cells, size_z), F32), jax.ShapeDtypeStruct((count_d, width), jnp.int32)),
        in_specs=[inside] * 7,
        out_specs=(anywhere, inside),
        scratch_shapes=[
            VMEM(padded, F32),
            VMEM((group * high * 8, 128), F32),
            VMEM((group * high, 128), F32),
            staged[0],
            staged[0],
            pltpu.SemaphoreType.DMA((3 + size_z // 128,)),
        ],
        compiler_params=params,
        cost_estimate=pl.CostEstimate(flops=10**8, bytes_accessed=4 * 10**6, transcendentals=0),
        name="spread",
    )(slots, own, field, keep, give, arrived, jnp.asarray(np.tile(shifts().T, (2, 1))))
    force = pl.pallas_call(
        functools.partial(owner_kernel, dims),
        out_shape=jax.ShapeDtypeStruct((3, count_d, width), F32),
        in_specs=[inside] * (4 + count_d // 2),
        out_specs=inside,
        scratch_shapes=[VMEM((count_d, high, 128), BF16)],
        compiler_params=params,
        name="owner",
    )(live, wanted, block_w, keep, first, *received)
    return out.reshape(velocity.shape), jnp.transpose(force, (1, 0, 2))[None, None]


def solution(mesh):
    return jax.shard_map(
        shards,
        mesh=mesh,
        in_specs=(
            P(None, "gx", "gy", None),
            P("gx", "gy", None, None, None, None),
            P("gx", "gy", None, None, None),
            P("gx", "gy", None, None),
            P("gx", "gy", None, None),
        ),
        out_specs=(P(None, "gx", "gy", None), P("gx", "gy", None, None, None)),
        check_vma=False,
    )
```
